32 devices in a mesh: groups: 2 (over x), gx: 16 (over z, y, core).
Axes of the slice: x: 2, y: 2, z: 4, core: 2. Of those that a mesh axis runs over, the one named last changes fastest.
Arguments:
- checkpoint: float32 [19, 64, 128, 128], P(None, 'gx', 'groups'), parts along dimension 2, as said below
- adjoint_seed: float32 [19, 64, 128, 128], P(None, 'gx', 'groups'), parts along dimension 2, may hold values from -6 to 6
- material: int32 [64, 128, 128], P('gx', 'groups'), parts along dimension 1, may hold values from 0 to 7
- wall_mask: int32 [64, 128, 128], P('gx', 'groups'), parts along dimension 1, may hold values from 0 to 1, as said below
- class_porosity: float32 [8], replicated, may hold values from 0.3 to 1
- step_index: int32 [2], P('groups'), parts along dimension 0, may hold values from 0 to 999
Outputs:
- adjoint_states: float32 [19, 64, 128, 128], P(None, 'gx', 'groups'), parts along dimension 2
- porosity_grad: float32 [64, 128, 128], P('gx', 'groups'), parts along dimension 1
The draws below stay inside these ranges and needn't reach their ends.
There are 2 independent parts, one for each index of `groups`. The reference program is written for one: setup_inputs(seed, part) draws one part's arguments, and reference() takes and returns one part's arrays. A program takes and returns all parts, laid end to end along the dimension named above; an argument that names none is the same for every part. Nothing has to cross between parts.
Inputs may be any that keep to these rules, and one draw needn't show every extreme that they name: `wall_mask`: cells at z = 0 and z = 127 are walls. `checkpoint`: populations are positive, with density near 1.
All inputs are finite; a program needn't handle non-finite values.
Results may differ from the reference program's by a relative error of at most 0.0003.
Values sent between devices are 32-bit elements; how exact they have to be, the bound alone decides.
A program may use at most 64 MiB of HBM per device.

```python
import jax
import jax.numpy as jnp
import numpy as np
from jax import lax

NY = 64
NZ = 128
Q = 19
NCLASS = 8
NX = 64


def draw_checkpoint(key, part):
    key = jax.random.fold_in(key, 11)
    keys = jax.random.split(key, 3)
    velocity_rows = [(0, 0, 0), (1, 0, 0), (-1, 0, 0), (0, 1, 0), (0, -1, 0), (0, 0, 1), (0, 0, -1), (1, 1, 0), (1, -1, 0), (-1, 1, 0), (-1, -1, 0), (1, 0, 1), (1, 0, -1), (-1, 0, 1), (-1, 0, -1), (0, 1, 1), (0, 1, -1), (0, -1, 1), (0, -1, -1)]
    vel_table = jnp.asarray(np.array(velocity_rows, dtype=np.float32))
    weight_col = jnp.asarray(np.array([1.0 / 3.0] + [1.0 / 18.0] * 6 + [1.0 / 36.0] * 12, dtype=np.float32))[:, None, None, None]
    flow = jnp.clip(0.03 * jax.random.normal(keys[0], (3, NX, NY, NZ), jnp.float32), -0.07, 0.07)
    density = 1.0 + jnp.clip(0.04 * jax.random.normal(keys[1], (NX, NY, NZ), jnp.float32), -0.1, 0.1)
    noise = jnp.clip(0.04 * jax.random.normal(keys[2], (19, NX, NY, NZ), jnp.float32), -0.08, 0.08)
    along = vel_table[:, 0, None, None, None] * flow[0][None] + vel_table[:, 1, None, None, None] * flow[1][None] + vel_table[:, 2, None, None, None] * flow[2][None]
    return weight_col * density[None] * (1.0 + 3.0 * along + noise)


def draw_wall_mask(key, part):
    key = jax.random.fold_in(key, 23)
    solid = jnp.where(jax.random.randint(key, (NX, NY, NZ), 0, 16) == 0, 1, 0)
    depth = jnp.arange(NZ, dtype=jnp.int32)[None, None, :]
    plates = jnp.where((depth == 0) | (depth == NZ - 1), 1, 0)
    return jnp.maximum(solid, plates).astype(jnp.int32)


def touch_ends(values, own_key, low, top_value):
    extent = values.shape
    place = [jax.random.randint(jax.random.fold_in(own_key, axis), (), 0, extent[axis]) for axis in range(len(extent))]
    values = values.at[tuple(place)].set(low)
    longest = extent.index(max(extent))
    place[longest] = (place[longest] + 1) % extent[longest]
    return values.at[tuple(place)].set(top_value)


def steps_of(key, extent, pieces, least, high):
    level = 1.0
    for axis_at, shards_of in pieces:
        draws = jax.random.uniform(jax.random.fold_in(jax.random.fold_in(key, 6), axis_at), (shards_of,), jnp.float32, least / len(pieces), high / len(pieces))
        level = level * jnp.repeat(jnp.exp(draws), extent[axis_at] // shards_of).reshape((-1,) + (1,) * (len(extent) - 1 - axis_at))
    return level


def scatter_about(key, dims, spread, reach, pieces=(), kind=jnp.bfloat16):
    factor_of = steps_of(key, dims, pieces, -0.22, 0.18) if pieces else 1.0
    result = jax.random.normal(key, dims, jnp.float32) * spread * factor_of
    return jnp.minimum(jnp.maximum(result, -reach), reach).astype(kind)


def setup_inputs(seed: int = 0, part: int = 0) -> dict:
    splits = jax.random.split(jax.random.key(seed), 7)
    part_keys = jax.random.split(jax.random.fold_in(splits[6], part), 7)
    checkpoint = draw_checkpoint(jax.random.fold_in(jax.random.fold_in(splits[6], part), 71), part)
    adjoint_seed = scatter_about(part_keys[1], (Q, NX, NY, NZ), 1.0, 6.0, ((1, 16),), jnp.float32)
    material = touch_ends(jax.random.randint(part_keys[2], (NX, NY, NZ), 0, NCLASS), jax.random.fold_in(part_keys[2], 1), 0, NCLASS - 1).astype(jnp.int32)
    wall_mask = draw_wall_mask(jax.random.fold_in(jax.random.fold_in(splits[6], part), 71), part)
    class_porosity = jnp.clip(jax.random.uniform(splits[4], (NCLASS,), jnp.float32, 0.3, 1.0), 0.3, 1.0)
    step_index = jax.random.randint(part_keys[5], (1,), 0, 1000).astype(jnp.int32)
    return {"checkpoint": checkpoint, "adjoint_seed": adjoint_seed, "material": material, "wall_mask": wall_mask, "class_porosity": class_porosity, "step_index": step_index}


def invert_matrix(matrix_rows):
    count_rows = len(matrix_rows)
    augmented = [list(matrix_rows[row_pos]) + [1.0 if row_pos == other else 0.0 for other in range(count_rows)] for row_pos in range(count_rows)]
    for column in range(count_rows):
        pivot_row = max(range(column, count_rows), key=lambda row_pos: abs(augmented[row_pos][column]))
        augmented[column], augmented[pivot_row] = (augmented[pivot_row], augmented[column])
        pivot_value = augmented[column][column]
        augmented[column] = [entry / pivot_value for entry in augmented[column]]
        for row_pos in range(count_rows):
            if row_pos != column:
                factor = augmented[row_pos][column]
                if factor != 0.0:
                    augmented[row_pos] = [left - factor * right for left, right in zip(augmented[row_pos], augmented[column])]
    return [entries[count_rows:] for entries in augmented]

def lattice_tables():
    velocity_rows = [(0, 0, 0)]
    for axis_pos in range(3):
        for sign_value in (1, -1):
            entry = [0, 0, 0]
            entry[axis_pos] = sign_value
            velocity_rows.append(tuple(entry))
    for first_axis, second_axis in ((0, 1), (0, 2), (1, 2)):
        for sign_one in (1, -1):
            for sign_two in (1, -1):
                entry = [0, 0, 0]
                entry[first_axis] = sign_one
                entry[second_axis] = sign_two
                velocity_rows.append(tuple(entry))
    opposite = [velocity_rows.index((-a, -b, -c)) for a, b, c in velocity_rows]
    weight_list = [1.0 / 3.0] + [1.0 / 18.0] * 6 + [1.0 / 36.0] * 12
    per_velocity = []
    for a, b, c in velocity_rows:
        a, b, c = (float(a), float(b), float(c))
        per_velocity.append([1.0, a, b, c, a * b, a * c, b * c, a * a, b * b, c * c, a * b * b, a * c * c, b * a * a, c * a * a, b * c * c, c * b * b, a * a * b * b, a * a * c * c, b * b * c * c])
    moments = [[per_velocity[popul][moment] for popul in range(19)] for moment in range(19)]
    rates = [0.0] * 4 + [1.6] * 6 + [1.4] * 6 + [1.2] * 3
    inverse = invert_matrix(moments)
    kernel_rows = [[sum((inverse[row_pos][inner] * rates[inner] * moments[inner][column] for inner in range(19))) for column in range(19)] for row_pos in range(19)]
    velocities = np.array(velocity_rows, dtype=np.int32)
    weights = np.array(weight_list, dtype=np.float32)
    kernel = np.array(kernel_rows, dtype=np.float32)
    return (velocities, weights, opposite, kernel)

def collide(states, porosity, wall_mask, force):
    velocities, weights, opposite, kernel = lattice_tables()
    highest = lax.Precision.HIGHEST
    vel_table = jnp.asarray(velocities.astype(np.float32))
    weight_col = jnp.asarray(weights)[:, None, None, None]
    density = lax.optimization_barrier(jnp.sum(states, 0))
    momentum = jnp.einsum('qa,qxyz->axyz', vel_table, states, precision=highest)
    flow = porosity[None] * momentum / density[None]
    along = jnp.einsum('qa,axyz->qxyz', vel_table, flow, precision=highest)
    square = lax.optimization_barrier(jnp.sum(flow * flow, 0))
    equilibrium = weight_col * density[None] * (1.0 + 3.0 * along + 4.5 * along * along - 1.5 * square[None])
    relaxed = states - jnp.einsum('qp,pxyz->qxyz', jnp.asarray(kernel), states - equilibrium, precision=highest)
    push_x = jnp.asarray((3.0 * weights * velocities[:, 0].astype(np.float32)).astype(np.float32))[:, None, None, None]
    relaxed = relaxed + push_x * force
    bounced = jnp.stack([states[opposite[popul]] for popul in range(19)])
    return jnp.where(wall_mask[None] == 1, bounced, relaxed)

def stream_all(relaxed, sign_value):
    velocities = lattice_tables()[0]
    return jnp.stack([jnp.roll(relaxed[popul], tuple((int(sign_value * velocities[popul, k]) for k in range(3))), axis=(0, 1, 2)) for popul in range(19)])

def reference(checkpoint, adjoint_seed, material, wall_mask, class_porosity, step_index):
    classes = jnp.arange(NCLASS, dtype=jnp.int32)[:, None, None, None]
    porosity = lax.optimization_barrier(jnp.sum(jnp.where(material[None] == classes, class_porosity[:, None, None, None], 0.0), 0))
    base_step = step_index[0].astype(jnp.float32)
    force_zero = 0.05 * jnp.sin(2.0 * jnp.pi * base_step / 64.0)
    force_one = 0.05 * jnp.sin(2.0 * jnp.pi * (base_step + 1.0) / 64.0)
    first = stream_all(collide(checkpoint, porosity, wall_mask, force_zero), 1)
    pulled_two = stream_all(adjoint_seed, -1)
    _, back_one = jax.vjp(lambda states, poros: collide(states, poros, wall_mask, force_one), first, porosity)
    adjoint_one, grad_two = back_one(pulled_two)
    pulled_one = stream_all(adjoint_one, -1)
    _, back_zero = jax.vjp(lambda states, poros: collide(states, poros, wall_mask, force_zero), checkpoint, porosity)
    adjoint_states, grad_one = back_zero(pulled_one)
    return (adjoint_states, grad_one + grad_two)
```

```python
import functools

import jax
import jax.numpy as jnp
import numpy as np
from jax import lax
from jax.experimental import pallas as pl
from jax.experimental.pallas import tpu as pltpu
from jax.sharding import PartitionSpec as P

MESH = pl.DeviceIdType.MESH
ROWS = 8


def velocity_list():
    rows = [(0, 0, 0)]
    for axis in range(3):
        for sign in (1, -1):
            entry = [0, 0, 0]
            entry[axis] = sign
            rows.append(tuple(entry))
    for first, second in ((0, 1), (0, 2), (1, 2)):
        for one in (1, -1):
            for two in (1, -1):
                entry = [0, 0, 0]
                entry[first] = one
                entry[second] = two
                rows.append(tuple(entry))
    return rows


VEL = velocity_list()
PLUS = [q for q in range(19) if VEL[q][0] == 1]
MINUS = [q for q in range(19) if VEL[q][0] == -1]
REST = [q for q in range(19) if VEL[q][0] == 0]
SLOT = {q: pos for pos, q in enumerate(PLUS + MINUS + REST)}
SAME = {q: q for q in range(19)}
AXIS = [(VEL.index(tuple(int(a == d) for d in range(3))),
         VEL.index(tuple(-int(a == d) for d in range(3)))) for a in range(3)]
PLANES = ((0, 1), (0, 2), (1, 2))


def corner(plane, one, two):
    entry = [0, 0, 0]
    entry[plane[0]] = one
    entry[plane[1]] = two
    return VEL.index(tuple(entry))


def to_pairs(f):
    sums = [f[p] + f[m] for p, m in AXIS]
    diffs = [f[p] - f[m] for p, m in AXIS]
    quads = []
    for plane in PLANES:
        pp, pm = f[corner(plane, 1, 1)], f[corner(plane, 1, -1)]
        mp, mm = f[corner(plane, -1, 1)], f[corner(plane, -1, -1)]
        s1, d1, s2, d2 = pp + pm, pp - pm, mp + mm, mp - mm
        quads.append((s1 + s2, d1 - d2, s1 - s2, d1 + d2))
    return f[0], sums, diffs, quads


def from_pairs(rest, sums, diffs, quads):
    out = {0: rest}
    for a, (p, m) in enumerate(AXIS):
        out[p] = sums[a] + diffs[a]
        out[m] = sums[a] - diffs[a]
    for plane, (qa, qb, qc, qd) in zip(PLANES, quads):
        s1, s2, d1, d2 = qa + qc, qa - qc, qb + qd, qd - qb
        out[corner(plane, 1, 1)] = s1 + d1
        out[corner(plane, 1, -1)] = s1 - d1
        out[corner(plane, -1, 1)] = s2 + d2
        out[corner(plane, -1, -1)] = s2 - d2
    return out


def conserved(rest, sums, diffs, quads):
    axy, axz, ayz = quads[0][0], quads[1][0], quads[2][0]
    density = (rest + (sums[0] + sums[1])) + (sums[2] + axy) + (axz + ayz)
    jx = diffs[0] + (quads[0][2] + quads[1][2])
    jy = diffs[1] + (quads[0][3] + quads[2][2])
    jz = diffs[2] + (quads[1][3] + quads[2][3])
    return density, (jx, jy, jz)


def rates(wall):
    pick = lambda at_wall, inside: jnp.where(wall, jnp.float32(at_wall), jnp.float32(inside))
    return dict(k2=pick(1, -0.6), s2=pick(0, 1.6), k3=pick(-1, -0.4), s3=pick(0, 1.4 / 3.0),
                k4=pick(1, -0.2), s4=pick(0, 1.2), sg=pick(-1, 1))


def forward(f, porosity, wall, force):
    k = rates(wall)
    rest, sums, diffs, quads = to_pairs(f)
    density, j = conserved(rest, sums, diffs, quads)
    ratio = porosity / density
    q = [porosity * c for c in j]
    u = [ratio * c for c in j]
    pxx, pyy, pzz = [q[a] * u[a] for a in range(3)]
    push = jnp.where(wall, 0.0, force)
    push3 = push * (1.0 / 3.0)
    third = density * (1.0 / 3.0)
    ninth = density * (1.0 / 9.0)
    a_of = [quads[n][0] for n in range(3)]
    even = [ninth + (pxx + pyy) * (1.0 / 3.0) - pzz * (1.0 / 6.0),
            ninth + (pxx + pzz) * (1.0 / 3.0) - pyy * (1.0 / 6.0),
            ninth + (pyy + pzz) * (1.0 / 3.0) - pxx * (1.0 / 6.0)]
    m = [sums[0] + (a_of[0] + a_of[1]), sums[1] + (a_of[0] + a_of[2]), sums[2] + (a_of[1] + a_of[2])]
    ms = [k["k2"] * m[a] + k["s2"] * (third + p) for a, p in enumerate((pxx, pyy, pzz))]
    new = []
    odd = [k["s3"] * q[0] + push3, k["s3"] * q[1], k["s3"] * q[2]]
    for n, (a, b) in enumerate(PLANES):
        qa, qb, qc, qd = quads[n]
        new.append((k["k4"] * qa + k["s4"] * even[n],
                    k["k2"] * qb + k["s2"] * (q[a] * u[b]),
                    k["k3"] * qc + odd[a],
                    k["k3"] * qd + odd[b]))
    axy, axz, ayz = new[0][0], new[1][0], new[2][0]
    s_new = [ms[0] - (axy + axz), ms[1] - (axy + ayz), ms[2] - (axz + ayz)]
    d_new = [(k["sg"] * j[0] + push) - (new[0][2] + new[1][2]),
             k["sg"] * j[1] - (new[0][3] + new[2][2]),
             k["sg"] * j[2] - (new[1][3] + new[2][3])]
    rest_new = density - (ms[0] + ms[1] + ms[2]) + (axy + axz + ayz)
    out = from_pairs(rest_new, [0.5 * s for s in s_new], [0.5 * d for d in d_new],
                     [tuple(0.25 * v for v in quad) for quad in new])
    return out, j, ratio


def backward(h, j, ratio, porosity, wall):
    k = rates(wall)
    h0, hs, hd, hq = to_pairs(h)
    hs = [0.5 * v for v in hs]
    hd = [0.5 * v for v in hd]
    hq = [tuple(0.25 * v for v in quad) for quad in hq]
    u = [ratio * c for c in j]
    ts = [v - h0 for v in hs]
    ta = [hq[n][0] - h0 - (ts[a] + ts[b]) for n, (a, b) in enumerate(PLANES)]
    tc = [(hq[n][2] - hd[a], hq[n][3] - hd[b]) for n, (a, b) in enumerate(PLANES)]
    ea = [k["s4"] * v for v in ta]
    eb = [k["s2"] * quad[1] for quad in hq]
    em = [k["s2"] * v for v in ts]
    px = em[0] + (ea[0] + ea[1]) * (1.0 / 3.0) - ea[2] * (1.0 / 6.0)
    py = em[1] + (ea[0] + ea[2]) * (1.0 / 3.0) - ea[1] * (1.0 / 6.0)
    pz = em[2] + (ea[1] + ea[2]) * (1.0 / 3.0) - ea[0] * (1.0 / 6.0)
    gx = 2.0 * px * u[0] + (eb[0] * u[1] + eb[1] * u[2])
    gy = 2.0 * py * u[1] + (eb[0] * u[0] + eb[2] * u[2])
    gz = 2.0 * pz * u[2] + (eb[1] * u[0] + eb[2] * u[1])
    a_rho = (h0 + (em[0] + em[1] + em[2]) * (1.0 / 3.0) + (ea[0] + ea[1] + ea[2]) * (1.0 / 9.0)
             - 0.5 * (u[0] * gx + u[1] * gy + u[2] * gz))
    g = [gx + k["s3"] * (tc[0][0] + tc[1][0]),
         gy + k["s3"] * (tc[0][1] + tc[2][0]),
         gz + k["s3"] * (tc[1][1] + tc[2][1])]
    grad = j[0] * g[0] + j[1] * g[1] + j[2] * g[2]
    aj = [k["sg"] * hd[a] + porosity * g[a] for a in range(3)]
    am = [k["k2"] * v for v in ts]
    quads = []
    for n, (a, b) in enumerate(PLANES):
        quads.append((k["k4"] * ta[n] + a_rho + (am[a] + am[b]),
                      k["k2"] * hq[n][1],
                      k["k3"] * tc[n][0] + aj[a],
                      k["k3"] * tc[n][1] + aj[b]))
    out = from_pairs(a_rho, [a_rho + v for v in am], aj, quads)
    return out, grad


def kernel(axis, poro_ref, step_ref, chk_hbm, seed_hbm, mat_hbm, wall_hbm, out_hbm, grad_hbm,
           chk, mat, wal, seed, post, adj, mom, por, out, grad,
           load_sem, send_sem, recv_sem, out_sem):
    width, ny, nz = mat.shape
    steps = ny // ROWS
    count = lax.axis_size(axis)
    me = lax.axis_index(axis)
    right, left = lax.rem(me + 1, count), lax.rem(me + count - 1, count)
    last = width - 1
    edge = [0, last] if width > 1 else [0]
    inner = max(width - 2, 0)

    barrier = pltpu.get_barrier_semaphore()
    for neighbour in (left, right):
        pl.semaphore_signal(barrier, inc=1, device_id={axis: neighbour}, device_id_type=MESH)

    loads = [pltpu.make_async_copy(mat_hbm, mat, load_sem.at[0]),
             pltpu.make_async_copy(wall_hbm, wal, load_sem.at[1])]
    edge_loads = [pltpu.make_async_copy(chk_hbm.at[:, x], chk.at[:, x], load_sem.at[2 + n])
                  for n, x in enumerate(edge)]
    late = []
    if inner:
        late.append(pltpu.make_async_copy(chk_hbm.at[:, pl.ds(1, inner)], chk.at[:, pl.ds(1, inner)],
                                          load_sem.at[4]))
    seed_load = pltpu.make_async_copy(seed_hbm, seed.at[:, pl.ds(1, width)], load_sem.at[5])
    for copy in loads + edge_loads + late + [seed_load]:
        copy.start()

    def remote(src, dst, number, target):
        return pltpu.make_async_remote_copy(
            src_ref=src, dst_ref=dst, send_sem=send_sem.at[number], recv_sem=recv_sem.at[number],
            device_id={axis: target}, device_id_type=MESH)

    seed_sends = []
    for start, size in ((1, 1), (7, 2), (11, 2)):
        seed_sends.append(remote(seed_hbm.at[pl.ds(start, size), 0],
                                 seed.at[pl.ds(start, size), width + 1], len(seed_sends), left))
    for start, size in ((2, 1), (9, 2), (13, 2)):
        seed_sends.append(remote(seed_hbm.at[pl.ds(start, size), last],
                                 seed.at[pl.ds(start, size), 0], len(seed_sends), right))
    post_up = remote(post.at[pl.ds(0, 5), width], post.at[pl.ds(0, 5), 0], 6, right)
    post_down = remote(post.at[pl.ds(5, 5), 1], post.at[pl.ds(5, 5), width + 1], 7, left)
    adj_down = remote(adj.at[pl.ds(0, 5), 1], adj.at[pl.ds(0, 5), width + 1], 8, left)
    adj_up = remote(adj.at[pl.ds(5, 5), width], adj.at[pl.ds(5, 5), 0], 9, right)

    row = lax.broadcasted_iota(jnp.int32, (ROWS, nz), 0)
    turn = (step_ref[0] & 63).astype(jnp.float32) * np.float32(2.0 * np.pi / 64.0)
    force = 0.05 * jnp.sin(jnp.full((ROWS, nz), turn, jnp.float32))

    def shifted(ref, slot, layer, i, sy, sz):
        value = ref[slot, layer, pl.ds(pl.multiple_of(i * ROWS, ROWS), ROWS), :]
        if sy:
            near = lax.rem(i + (steps - 1 if sy > 0 else 1), steps)
            other = ref[slot, layer, pl.ds(pl.multiple_of(near * ROWS, ROWS), ROWS), :]
            value = jnp.where(row == (ROWS - 1 if sy > 0 else 0), other, value)
            value = pltpu.roll(value, sy % ROWS, 0)
        if sz:
            value = pltpu.roll(value, sz % nz, 1)
        return value

    def streamed(ref, x, i, sign, slots):
        return [shifted(ref, slots[q], x + 1 - sign * VEL[q][0], i, sign * VEL[q][1],
                        sign * VEL[q][2]) for q in range(19)]

    def over(layers, body):
        first, stride, number = layers
        if number == 0:
            return

        def step(t, carry):
            body(first + stride * (t // steps), lax.rem(t, steps))
            return carry

        lax.fori_loop(0, number * steps, step, 0)

    edges = (0, max(last, 1), len(edge))
    middle = (1, 1, inner)

    def here(i):
        return pl.ds(pl.multiple_of(i * ROWS, ROWS), ROWS)

    def collide(x, i):
        at = here(i)
        kinds = mat[x, at, :]
        porosity = jnp.zeros((ROWS, nz), jnp.float32)
        for number in range(poro_ref.shape[0]):
            porosity = jnp.where(kinds == number, poro_ref[number], porosity)
        f = [chk[q, x, at, :] for q in range(19)]
        g, j, ratio = forward(f, porosity, wal[x, at, :] == 1, force)
        for q in range(19):
            post[SLOT[q], x + 1, at, :] = g[q]
        por[x, at, :] = porosity
        for n, value in enumerate((*j, ratio)):
            mom[n, x, at, :] = value

    def back_one(x, i):
        at = here(i)
        porosity = por[x, at, :]
        density, j = conserved(*to_pairs(streamed(post, x, i, 1, SLOT)))
        h = streamed(seed, x, i, -1, SAME)
        a, part = backward(h, j, porosity / density, porosity, wal[x, at, :] == 1)
        for q in range(19):
            adj[SLOT[q], x + 1, at, :] = a[q]
        grad[x, at, :] = part

    def back_zero(x, i):
        at = here(i)
        h = streamed(adj, x, i, -1, SLOT)
        j = [mom[n, x, at, :] for n in range(3)]
        a, part = backward(h, j, mom[3, x, at, :], por[x, at, :], wal[x, at, :] == 1)
        for q in range(19):
            out[q, x, at, :] = a[q]
        grad[x, at, :] = grad[x, at, :] + part

    pl.semaphore_wait(barrier, 2)
    for copy in seed_sends:
        copy.start()
    for copy in loads + edge_loads:
        copy.wait()
    over(edges, collide)
    post_up.start()
    post_down.start()
    for copy in late:
        copy.wait()
    over(middle, collide)
    seed_load.wait()
    over(middle, back_one)
    for copy in seed_sends + [post_up, post_down]:
        copy.wait_recv()
    over(edges, back_one)
    adj_up.start()
    adj_down.start()
    over(middle, back_zero)
    stores = []
    if inner:
        stores.append(pltpu.make_async_copy(out.at[:, pl.ds(1, inner)], out_hbm.at[:, pl.ds(1, inner)],
                                            out_sem.at[0]))
        stores[-1].start()
    adj_up.wait_recv()
    adj_down.wait_recv()
    over(edges, back_zero)
    for n, x in enumerate(edge):
        stores.append(pltpu.make_async_copy(out.at[:, x], out_hbm.at[:, x], out_sem.at[1 + n]))
    stores.append(pltpu.make_async_copy(grad, grad_hbm, out_sem.at[3]))
    for copy in stores[-1 - len(edge):]:
        copy.start()
    for copy in seed_sends + [post_up, post_down, adj_up, adj_down]:
        copy.wait_send()
    for copy in stores:
        copy.wait()


def local(checkpoint, adjoint_seed, material, wall_mask, class_porosity, step_index):
    width, ny, nz = material.shape
    f32 = jnp.float32
    anywhere = pl.BlockSpec(memory_space=pl.ANY)
    scalars = pl.BlockSpec(memory_space=pltpu.SMEM)
    return pl.pallas_call(
        functools.partial(kernel, "gx"),
        out_shape=(jax.ShapeDtypeStruct(checkpoint.shape, f32),
                   jax.ShapeDtypeStruct(material.shape, f32)),
        in_specs=[scalars, scalars] + [anywhere] * 4,
        out_specs=(anywhere, anywhere),
        scratch_shapes=[
            pltpu.VMEM((19, width, ny, nz), f32),
            pltpu.VMEM((width, ny, nz), jnp.int32),
            pltpu.VMEM((width, ny, nz), jnp.int32),
            pltpu.VMEM((19, width + 2, ny, nz), f32),
            pltpu.VMEM((19, width + 2, ny, nz), f32),
            pltpu.VMEM((19, width + 2, ny, nz), f32),
            pltpu.VMEM((4, width, ny, nz), f32),
            pltpu.VMEM((width, ny, nz), f32),
            pltpu.VMEM((19, width, ny, nz), f32),
            pltpu.VMEM((width, ny, nz), f32),
            pltpu.SemaphoreType.DMA((6,)),
            pltpu.SemaphoreType.DMA((10,)),
            pltpu.SemaphoreType.DMA((10,)),
            pltpu.SemaphoreType.DMA((4,)),
        ],
        compiler_params=pltpu.CompilerParams(
            collective_id=0, has_side_effects=True, vmem_limit_bytes=44 * 2**20),
    )(class_porosity, step_index, checkpoint, adjoint_seed, material, wall_mask)


def solution(mesh):
    placed = (
        P(None, "gx", "groups", None),
        P(None, "gx", "groups", None),
        P("gx", "groups", None),
        P("gx", "groups", None),
        P(),
        P("groups"),
    )
    return jax.shard_map(
        local,
        mesh=mesh,
        in_specs=placed,
        out_specs=(P(None, "gx", "groups", None), P("gx", "groups", None)),
        check_vma=False,
    )
```

```python
import functools

import jax
import jax.numpy as jnp
import numpy as np
from jax import lax
from jax.experimental import pallas as pl
from jax.experimental.pallas import tpu as pltpu
from jax.sharding import PartitionSpec as P

MESH = pl.DeviceIdType.MESH
ROWS = 8
UNROLL = 4


def velocity_list():
    rows = [(0, 0, 0)]
    for axis in range(3):
        for sign in (1, -1):
            entry = [0, 0, 0]
            entry[axis] = sign
            rows.append(tuple(entry))
    for first, second in ((0, 1), (0, 2), (1, 2)):
        for one in (1, -1):
            for two in (1, -1):
                entry = [0, 0, 0]
                entry[first] = one
                entry[second] = two
                rows.append(tuple(entry))
    return rows


VEL = velocity_list()
PLUS = [q for q in range(19) if VEL[q][0] == 1]
MINUS = [q for q in range(19) if VEL[q][0] == -1]
REST = [q for q in range(19) if VEL[q][0] == 0]
SLOT = {q: pos for pos, q in enumerate(PLUS + MINUS + REST)}
SAME = {q: q for q in range(19)}
AXIS = [(VEL.index(tuple(int(a == d) for d in range(3))),
         VEL.index(tuple(-int(a == d) for d in range(3)))) for a in range(3)]
PLANES = ((0, 1), (0, 2), (1, 2))


def corner(plane, one, two):
    entry = [0, 0, 0]
    entry[plane[0]] = one
    entry[plane[1]] = two
    return VEL.index(tuple(entry))


def to_pairs(f):
    sums = [f[p] + f[m] for p, m in AXIS]
    diffs = [f[p] - f[m] for p, m in AXIS]
    quads = []
    for plane in PLANES:
        pp, pm = f[corner(plane, 1, 1)], f[corner(plane, 1, -1)]
        mp, mm = f[corner(plane, -1, 1)], f[corner(plane, -1, -1)]
        s1, d1, s2, d2 = pp + pm, pp - pm, mp + mm, mp - mm
        quads.append((s1 + s2, d1 - d2, s1 - s2, d1 + d2))
    return f[0], sums, diffs, quads


def from_pairs(rest, sums, diffs, quads):
    out = {0: rest}
    for a, (p, m) in enumerate(AXIS):
        out[p] = sums[a] + diffs[a]
        out[m] = sums[a] - diffs[a]
    for plane, (qa, qb, qc, qd) in zip(PLANES, quads):
        s1, s2, d1, d2 = qa + qc, qa - qc, qb + qd, qd - qb
        out[corner(plane, 1, 1)] = s1 + d1
        out[corner(plane, 1, -1)] = s1 - d1
        out[corner(plane, -1, 1)] = s2 + d2
        out[corner(plane, -1, -1)] = s2 - d2
    return out


def conserved(rest, sums, diffs, quads):
    axy, axz, ayz = quads[0][0], quads[1][0], quads[2][0]
    density = (rest + (sums[0] + sums[1])) + (sums[2] + axy) + (axz + ayz)
    jx = diffs[0] + (quads[0][2] + quads[1][2])
    jy = diffs[1] + (quads[0][3] + quads[2][2])
    jz = diffs[2] + (quads[1][3] + quads[2][3])
    return density, (jx, jy, jz)


def rates(wall):
    pick = lambda at_wall, inside: jnp.where(wall, jnp.float32(at_wall), jnp.float32(inside))
    return dict(k2=pick(1, -0.6), s2=pick(0, 1.6), k3=pick(-1, -0.4), s3=pick(0, 1.4 / 3.0),
                k4=pick(1, -0.2), s4=pick(0, 1.2), sg=pick(-1, 1))


def forward(f, porosity, wall, force):
    k = rates(wall)
    rest, sums, diffs, quads = to_pairs(f)
    density, j = conserved(rest, sums, diffs, quads)
    ratio = porosity / density
    q = [porosity * c for c in j]
    u = [ratio * c for c in j]
    pxx, pyy, pzz = [q[a] * u[a] for a in range(3)]
    push = jnp.where(wall, 0.0, force)
    push3 = push * (1.0 / 3.0)
    third = density * (1.0 / 3.0)
    ninth = density * (1.0 / 9.0)
    a_of = [quads[n][0] for n in range(3)]
    even = [ninth + (pxx + pyy) * (1.0 / 3.0) - pzz * (1.0 / 6.0),
            ninth + (pxx + pzz) * (1.0 / 3.0) - pyy * (1.0 / 6.0),
            ninth + (pyy + pzz) * (1.0 / 3.0) - pxx * (1.0 / 6.0)]
    m = [sums[0] + (a_of[0] + a_of[1]), sums[1] + (a_of[0] + a_of[2]), sums[2] + (a_of[1] + a_of[2])]
    ms = [k["k2"] * m[a] + k["s2"] * (third + p) for a, p in enumerate((pxx, pyy, pzz))]
    new = []
    odd = [k["s3"] * q[0] + push3, k["s3"] * q[1], k["s3"] * q[2]]
    for n, (a, b) in enumerate(PLANES):
        qa, qb, qc, qd = quads[n]
        new.append((k["k4"] * qa + k["s4"] * even[n],
                    k["k2"] * qb + k["s2"] * (q[a] * u[b]),
                    k["k3"] * qc + odd[a],
                    k["k3"] * qd + odd[b]))
    axy, axz, ayz = new[0][0], new[1][0], new[2][0]
    s_new = [ms[0] - (axy + axz), ms[1] - (axy + ayz), ms[2] - (axz + ayz)]
    d_new = [(k["sg"] * j[0] + push) - (new[0][2] + new[1][2]),
             k["sg"] * j[1] - (new[0][3] + new[2][2]),
             k["sg"] * j[2] - (new[1][3] + new[2][3])]
    rest_new = density - (ms[0] + ms[1] + ms[2]) + (axy + axz + ayz)
    out = from_pairs(rest_new, [0.5 * s for s in s_new], [0.5 * d for d in d_new],
                     [tuple(0.25 * v for v in quad) for quad in new])
    return out, j, ratio


def backward(h, j, ratio, porosity, wall):
    k = rates(wall)
    h0, hs, hd, hq = to_pairs(h)
    hs = [0.5 * v for v in hs]
    hd = [0.5 * v for v in hd]
    hq = [tuple(0.25 * v for v in quad) for quad in hq]
    u = [ratio * c for c in j]
    ts = [v - h0 for v in hs]
    ta = [hq[n][0] - h0 - (ts[a] + ts[b]) for n, (a, b) in enumerate(PLANES)]
    tc = [(hq[n][2] - hd[a], hq[n][3] - hd[b]) for n, (a, b) in enumerate(PLANES)]
    ea = [k["s4"] * v for v in ta]
    eb = [k["s2"] * quad[1] for quad in hq]
    em = [k["s2"] * v for v in ts]
    px = em[0] + (ea[0] + ea[1]) * (1.0 / 3.0) - ea[2] * (1.0 / 6.0)
    py = em[1] + (ea[0] + ea[2]) * (1.0 / 3.0) - ea[1] * (1.0 / 6.0)
    pz = em[2] + (ea[1] + ea[2]) * (1.0 / 3.0) - ea[0] * (1.0 / 6.0)
    gx = 2.0 * px * u[0] + (eb[0] * u[1] + eb[1] * u[2])
    gy = 2.0 * py * u[1] + (eb[0] * u[0] + eb[2] * u[2])
    gz = 2.0 * pz * u[2] + (eb[1] * u[0] + eb[2] * u[1])
    a_rho = (h0 + (em[0] + em[1] + em[2]) * (1.0 / 3.0) + (ea[0] + ea[1] + ea[2]) * (1.0 / 9.0)
             - 0.5 * (u[0] * gx + u[1] * gy + u[2] * gz))
    g = [gx + k["s3"] * (tc[0][0] + tc[1][0]),
         gy + k["s3"] * (tc[0][1] + tc[2][0]),
         gz + k["s3"] * (tc[1][1] + tc[2][1])]
    grad = j[0] * g[0] + j[1] * g[1] + j[2] * g[2]
    aj = [k["sg"] * hd[a] + porosity * g[a] for a in range(3)]
    am = [k["k2"] * v for v in ts]
    quads = []
    for n, (a, b) in enumerate(PLANES):
        quads.append((k["k4"] * ta[n] + a_rho + (am[a] + am[b]),
                      k["k2"] * hq[n][1],
                      k["k3"] * tc[n][0] + aj[a],
                      k["k3"] * tc[n][1] + aj[b]))
    out = from_pairs(a_rho, [a_rho + v for v in am], aj, quads)
    return out, grad


def kernel(axis, poro_hbm, step_ref, chk_hbm, seed_hbm, mat_hbm, wall_hbm, out_hbm, grad_hbm,
           poro_ref, chk, mat, wal, seed, post, adj, mom, por, out, grad, face, halo,
           load_sem, send_sem, recv_sem, out_sem):
    width, ny, nz = mat.shape
    steps = ny // ROWS
    count = lax.axis_size(axis)
    me = lax.axis_index(axis)
    right, left = lax.rem(me + 1, count), lax.rem(me + count - 1, count)
    last = width - 1
    edge = [0, last] if width > 1 else [0]
    inner = max(width - 2, 0)

    barrier = pltpu.get_barrier_semaphore()
    for neighbour in (left, right):
        pl.semaphore_signal(barrier, inc=1, device_id={axis: neighbour}, device_id_type=MESH)

    loads = [pltpu.make_async_copy(mat_hbm, mat, load_sem.at[0]),
             pltpu.make_async_copy(wall_hbm, wal, load_sem.at[1])]
    edge_loads = [pltpu.make_async_copy(chk_hbm.at[:, x], chk.at[:, x], load_sem.at[2 + n])
                  for n, x in enumerate(edge)]
    late = []
    if inner:
        late.append(pltpu.make_async_copy(chk_hbm.at[:, pl.ds(1, inner)], chk.at[:, pl.ds(1, inner)],
                                          load_sem.at[4]))
    seed_load = pltpu.make_async_copy(seed_hbm, seed.at[:, pl.ds(1, width)], load_sem.at[5])
    loads.append(pltpu.make_async_copy(poro_hbm, poro_ref, load_sem.at[6]))
    for copy in loads + edge_loads + late + [seed_load]:
        copy.start()

    def remote(src, dst, number, target):
        return pltpu.make_async_remote_copy(
            src_ref=src, dst_ref=dst, send_sem=send_sem.at[number], recv_sem=recv_sem.at[number],
            device_id={axis: target}, device_id_type=MESH)

    seed_sends = []
    for start, size in ((1, 1), (7, 2), (11, 2)):
        seed_sends.append(remote(seed_hbm.at[pl.ds(start, size), 0],
                                 seed.at[pl.ds(start, size), width + 1], len(seed_sends), left))
    for start, size in ((2, 1), (9, 2), (13, 2)):
        seed_sends.append(remote(seed_hbm.at[pl.ds(start, size), last],
                                 seed.at[pl.ds(start, size), 0], len(seed_sends), right))
    post_up = remote(face.at[0], halo.at[0], 6, right)
    post_down = remote(face.at[1], halo.at[1], 7, left)
    adj_down = remote(adj.at[pl.ds(0, 5), 1], adj.at[pl.ds(0, 5), width + 1], 8, left)
    adj_up = remote(adj.at[pl.ds(5, 5), width], adj.at[pl.ds(5, 5), 0], 9, right)

    row = lax.broadcasted_iota(jnp.int32, (ROWS, nz), 0)

    def shifted(ref, slot, layer, i, sy, sz):
        value = ref[slot, layer, pl.ds(pl.multiple_of(i * ROWS, ROWS), ROWS), :]
        if sy:
            near = lax.rem(i + (steps - 1 if sy > 0 else 1), steps)
            other = ref[slot, layer, pl.ds(pl.multiple_of(near * ROWS, ROWS), ROWS), :]
            value = jnp.where(row == (ROWS - 1 if sy > 0 else 0), other, value)
            value = pltpu.roll(value, sy % ROWS, 0)
        if sz:
            value = pltpu.roll(value, sz % nz, 1)
        return value

    def streamed(ref, x, i, sign, slots, without=()):
        return [jnp.zeros((ROWS, nz), jnp.float32) if VEL[q][0] in without else
                shifted(ref, slots[q], x + 1 - sign * VEL[q][0], i, sign * VEL[q][1],
                        sign * VEL[q][2]) for q in range(19)]

    def over(layers, body):
        first, stride, number = layers
        if number == 0:
            return

        def step(t, carry):
            body(first + stride * (t // steps), lax.rem(t, steps))
            return carry

        lax.fori_loop(0, number * steps, step, 0, unroll=UNROLL)

    bottom, top = (0, 1, 1), (last, 1, 1)
    middle = (1, 1, inner)

    def here(i):
        return pl.ds(pl.multiple_of(i * ROWS, ROWS), ROWS)

    def collide(x, i):
        at = here(i)
        kinds = mat[x, at, :]
        porosity = jnp.zeros((ROWS, nz), jnp.float32)
        for number in range(poro_ref.shape[0]):
            porosity = jnp.where(kinds == number, poro_ref[number], porosity)
        f = [chk[q, x, at, :] for q in range(19)]
        g, j, ratio = forward(f, porosity, wal[x, at, :] == 1, force)
        for q in range(19):
            post[SLOT[q], x + 1, at, :] = g[q]
        por[x, at, :] = porosity
        for n, value in enumerate((*j, ratio)):
            mom[n, x, at, :] = value

    def fold(x, sign):
        def body(_, i):
            moved = {VEL[q][1:]: shifted(post, SLOT[q], x + 1, i, VEL[q][1], VEL[q][2])
                     for q in (PLUS if sign > 0 else MINUS)}
            up, down, fore, aft = moved[1, 0], moved[-1, 0], moved[0, 1], moved[0, -1]
            side = 0 if sign > 0 else 1
            face[side, 0, here(i), :] = moved[0, 0] + (up + down) + (fore + aft)
            face[side, 1, here(i), :] = up - down
            face[side, 2, here(i), :] = fore - aft
        return body

    def back_one(x, i, folded=()):
        at = here(i)
        porosity = por[x, at, :]
        first = streamed(post, x, i, 1, SLOT, [sign for sign, _ in folded])
        density, j = conserved(*to_pairs(first))
        for sign, side in folded:
            total = halo[side, 0, at, :]
            density = density + total
            j = (j[0] + sign * total, j[1] + halo[side, 1, at, :], j[2] + halo[side, 2, at, :])
        h = streamed(seed, x, i, -1, SAME)
        a, part = backward(h, j, porosity / density, porosity, wal[x, at, :] == 1)
        for q in range(19):
            adj[SLOT[q], x + 1, at, :] = a[q]
        grad[x, at, :] = part

    def at_bottom(x, i):
        back_one(x, i, ((1, 0),) if width > 1 else ((1, 0), (-1, 1)))

    def at_top(x, i):
        back_one(x, i, ((-1, 1),))

    def back_zero(x, i):
        at = here(i)
        h = streamed(adj, x, i, -1, SLOT)
        j = [mom[n, x, at, :] for n in range(3)]
        a, part = backward(h, j, mom[3, x, at, :], por[x, at, :], wal[x, at, :] == 1)
        for q in range(19):
            out[q, x, at, :] = a[q]
        grad[x, at, :] = grad[x, at, :] + part

    pl.semaphore_wait(barrier, 2)
    for copy in seed_sends:
        copy.start()
    for copy in loads:
        copy.wait()
    turn = (step_ref[0] & 63).astype(jnp.float32) * np.float32(2.0 * np.pi / 64.0)
    force = 0.05 * jnp.sin(jnp.full((ROWS, nz), turn, jnp.float32))
    edge_loads[0].wait()
    over(bottom, collide)
    over(bottom, fold(0, -1))
    post_down.start()
    if width > 1:
        edge_loads[1].wait()
        over(top, collide)
    over(top, fold(last, 1))
    post_up.start()
    for copy in late:
        copy.wait()
    over(middle, collide)
    seed_load.wait()
    over(middle, back_one)
    from_left, from_right = seed_sends[3:] + [post_up], seed_sends[:3] + [post_down]
    for copy in from_left if width > 1 else from_left + from_right:
        copy.wait_recv()
    over(bottom, at_bottom)
    adj_down.start()
    if width > 1:
        for copy in from_right:
            copy.wait_recv()
        over(top, at_top)
    adj_up.start()
    over(middle, back_zero)
    stores = []

    def store(x, size):
        stores.append(pltpu.make_async_copy(out.at[:, pl.ds(x, size)], out_hbm.at[:, pl.ds(x, size)],
                                            out_sem.at[len(stores)]))
        stores[-1].start()

    if inner:
        store(1, inner)
    adj_up.wait_recv()
    if width == 1:
        adj_down.wait_recv()
    over(bottom, back_zero)
    store(0, 1)
    if width > 1:
        adj_down.wait_recv()
        over(top, back_zero)
        store(last, 1)
    stores.append(pltpu.make_async_copy(grad, grad_hbm, out_sem.at[3]))
    stores[-1].start()
    for copy in seed_sends + [post_up, post_down, adj_up, adj_down]:
        copy.wait_send()
    for copy in stores:
        copy.wait()


def local(checkpoint, adjoint_seed, material, wall_mask, class_porosity, step_index):
    width, ny, nz = material.shape
    f32 = jnp.float32
    anywhere = pl.BlockSpec(memory_space=pltpu.HBM)
    scalars = pl.BlockSpec(memory_space=pltpu.SMEM)
    return pl.pallas_call(
        functools.partial(kernel, "gx"),
        out_shape=(jax.ShapeDtypeStruct(checkpoint.shape, f32),
                   jax.ShapeDtypeStruct(material.shape, f32)),
        in_specs=[anywhere, scalars] + [anywhere] * 4,
        out_specs=(anywhere, anywhere),
        scratch_shapes=[
            pltpu.SMEM(class_porosity.shape, f32),
            pltpu.VMEM((19, width, ny, nz), f32),
            pltpu.VMEM((width, ny, nz), jnp.int32),
            pltpu.VMEM((width, ny, nz), jnp.int32),
            pltpu.VMEM((19, width + 2, ny, nz), f32),
            pltpu.VMEM((19, width + 2, ny, nz), f32),
            pltpu.VMEM((19, width + 2, ny, nz), f32),
            pltpu.VMEM((4, width, ny, nz), f32),
            pltpu.VMEM((width, ny, nz), f32),
            pltpu.VMEM((19, width, ny, nz), f32),
            pltpu.VMEM((width, ny, nz), f32),
            pltpu.VMEM((2, 3, ny, nz), f32),
            pltpu.VMEM((2, 3, ny, nz), f32),
            pltpu.SemaphoreType.DMA((7,)),
            pltpu.SemaphoreType.DMA((10,)),
            pltpu.SemaphoreType.DMA((10,)),
            pltpu.SemaphoreType.DMA((4,)),
        ],
        compiler_params=pltpu.CompilerParams(
            collective_id=0, has_side_effects=True, vmem_limit_bytes=56 * 2**20),
    )(class_porosity, step_index, checkpoint, adjoint_seed, material, wall_mask)


def solution(mesh):
    placed = (
        P(None, "gx", "groups", None),
        P(None, "gx", "groups", None),
        P("gx", "groups", None),
        P("gx", "groups", None),
        P(),
        P("groups"),
    )
    return jax.shard_map(
        local,
        mesh=mesh,
        in_specs=placed,
        out_specs=(P(None, "gx", "groups", None), P("gx", "groups", None)),
        check_vma=False,
    )
```

```python
import functools

import jax
import jax.numpy as jnp
import numpy as np
from jax import lax
from jax.experimental import pallas as pl
from jax.experimental.pallas import tpu as pltpu
from jax.sharding import PartitionSpec as P

MESH = pl.DeviceIdType.MESH
ROWS = 8
UNROLL = 4


def velocity_list():
    rows = [(0, 0, 0)]
    for axis in range(3):
        for sign in (1, -1):
            entry = [0, 0, 0]
            entry[axis] = sign
            rows.append(tuple(entry))
    for first, second in ((0, 1), (0, 2), (1, 2)):
        for one in (1, -1):
            for two in (1, -1):
                entry = [0, 0, 0]
                entry[first] = one
                entry[second] = two
                rows.append(tuple(entry))
    return rows


VEL = velocity_list()
PLUS = [q for q in range(19) if VEL[q][0] == 1]
MINUS = [q for q in range(19) if VEL[q][0] == -1]
REST = [q for q in range(19) if VEL[q][0] == 0]
SLOT = {q: pos for pos, q in enumerate(PLUS + MINUS + REST)}
SAME = {q: q for q in range(19)}
AXIS = [(VEL.index(tuple(int(a == d) for d in range(3))),
         VEL.index(tuple(-int(a == d) for d in range(3)))) for a in range(3)]
PLANES = ((0, 1), (0, 2), (1, 2))


def corner(plane, one, two):
    entry = [0, 0, 0]
    entry[plane[0]] = one
    entry[plane[1]] = two
    return VEL.index(tuple(entry))


def to_pairs(f):
    sums = [f[p] + f[m] for p, m in AXIS]
    diffs = [f[p] - f[m] for p, m in AXIS]
    quads = []
    for plane in PLANES:
        pp, pm = f[corner(plane, 1, 1)], f[corner(plane, 1, -1)]
        mp, mm = f[corner(plane, -1, 1)], f[corner(plane, -1, -1)]
        s1, d1, s2, d2 = pp + pm, pp - pm, mp + mm, mp - mm
        quads.append((s1 + s2, d1 - d2, s1 - s2, d1 + d2))
    return f[0], sums, diffs, quads


def from_pairs(rest, sums, diffs, quads):
    out = {0: rest}
    for a, (p, m) in enumerate(AXIS):
        out[p] = sums[a] + diffs[a]
        out[m] = sums[a] - diffs[a]
    for plane, (qa, qb, qc, qd) in zip(PLANES, quads):
        s1, s2, d1, d2 = qa + qc, qa - qc, qb + qd, qd - qb
        out[corner(plane, 1, 1)] = s1 + d1
        out[corner(plane, 1, -1)] = s1 - d1
        out[corner(plane, -1, 1)] = s2 + d2
        out[corner(plane, -1, -1)] = s2 - d2
    return out


def conserved(rest, sums, diffs, quads):
    axy, axz, ayz = quads[0][0], quads[1][0], quads[2][0]
    density = (rest + (sums[0] + sums[1])) + (sums[2] + axy) + (axz + ayz)
    jx = diffs[0] + (quads[0][2] + quads[1][2])
    jy = diffs[1] + (quads[0][3] + quads[2][2])
    jz = diffs[2] + (quads[1][3] + quads[2][3])
    return density, (jx, jy, jz)


def rates(wall):
    pick = lambda at_wall, inside: jnp.where(wall, jnp.float32(at_wall), jnp.float32(inside))
    return dict(k2=pick(1, -0.6), s2=pick(0, 1.6), k3=pick(-1, -0.4), s3=pick(0, 1.4 / 3.0),
                k4=pick(1, -0.2), s4=pick(0, 1.2), sg=pick(-1, 1))


def forward(f, porosity, wall, force):
    k = rates(wall)
    rest, sums, diffs, quads = to_pairs(f)
    density, j = conserved(rest, sums, diffs, quads)
    ratio = porosity / density
    q = [porosity * c for c in j]
    u = [ratio * c for c in j]
    pxx, pyy, pzz = [q[a] * u[a] for a in range(3)]
    push = jnp.where(wall, 0.0, force)
    push3 = push * (1.0 / 3.0)
    third = density * (1.0 / 3.0)
    ninth = density * (1.0 / 9.0)
    a_of = [quads[n][0] for n in range(3)]
    even = [ninth + (pxx + pyy) * (1.0 / 3.0) - pzz * (1.0 / 6.0),
            ninth + (pxx + pzz) * (1.0 / 3.0) - pyy * (1.0 / 6.0),
            ninth + (pyy + pzz) * (1.0 / 3.0) - pxx * (1.0 / 6.0)]
    m = [sums[0] + (a_of[0] + a_of[1]), sums[1] + (a_of[0] + a_of[2]), sums[2] + (a_of[1] + a_of[2])]
    ms = [k["k2"] * m[a] + k["s2"] * (third + p) for a, p in enumerate((pxx, pyy, pzz))]
    new = []
    odd = [k["s3"] * q[0] + push3, k["s3"] * q[1], k["s3"] * q[2]]
    for n, (a, b) in enumerate(PLANES):
        qa, qb, qc, qd = quads[n]
        new.append((k["k4"] * qa + k["s4"] * even[n],
                    k["k2"] * qb + k["s2"] * (q[a] * u[b]),
                    k["k3"] * qc + odd[a],
                    k["k3"] * qd + odd[b]))
    axy, axz, ayz = new[0][0], new[1][0], new[2][0]
    s_new = [ms[0] - (axy + axz), ms[1] - (axy + ayz), ms[2] - (axz + ayz)]
    d_new = [(k["sg"] * j[0] + push) - (new[0][2] + new[1][2]),
             k["sg"] * j[1] - (new[0][3] + new[2][2]),
             k["sg"] * j[2] - (new[1][3] + new[2][3])]
    rest_new = density - (ms[0] + ms[1] + ms[2]) + (axy + axz + ayz)
    out = from_pairs(rest_new, [0.5 * s for s in s_new], [0.5 * d for d in d_new],
                     [tuple(0.25 * v for v in quad) for quad in new])
    return out, j, ratio


def backward(h, j, ratio, porosity, wall):
    k = rates(wall)
    h0, hs, hd, hq = to_pairs(h)
    hs = [0.5 * v for v in hs]
    hd = [0.5 * v for v in hd]
    hq = [tuple(0.25 * v for v in quad) for quad in hq]
    u = [ratio * c for c in j]
    ts = [v - h0 for v in hs]
    ta = [hq[n][0] - h0 - (ts[a] + ts[b]) for n, (a, b) in enumerate(PLANES)]
    tc = [(hq[n][2] - hd[a], hq[n][3] - hd[b]) for n, (a, b) in enumerate(PLANES)]
    ea = [k["s4"] * v for v in ta]
    eb = [k["s2"] * quad[1] for quad in hq]
    em = [k["s2"] * v for v in ts]
    px = em[0] + (ea[0] + ea[1]) * (1.0 / 3.0) - ea[2] * (1.0 / 6.0)
    py = em[1] + (ea[0] + ea[2]) * (1.0 / 3.0) - ea[1] * (1.0 / 6.0)
    pz = em[2] + (ea[1] + ea[2]) * (1.0 / 3.0) - ea[0] * (1.0 / 6.0)
    gx = 2.0 * px * u[0] + (eb[0] * u[1] + eb[1] * u[2])
    gy = 2.0 * py * u[1] + (eb[0] * u[0] + eb[2] * u[2])
    gz = 2.0 * pz * u[2] + (eb[1] * u[0] + eb[2] * u[1])
    a_rho = (h0 + (em[0] + em[1] + em[2]) * (1.0 / 3.0) + (ea[0] + ea[1] + ea[2]) * (1.0 / 9.0)
             - 0.5 * (u[0] * gx + u[1] * gy + u[2] * gz))
    g = [gx + k["s3"] * (tc[0][0] + tc[1][0]),
         gy + k["s3"] * (tc[0][1] + tc[2][0]),
         gz + k["s3"] * (tc[1][1] + tc[2][1])]
    grad = j[0] * g[0] + j[1] * g[1] + j[2] * g[2]
    aj = [k["sg"] * hd[a] + porosity * g[a] for a in range(3)]
    am = [k["k2"] * v for v in ts]
    quads = []
    for n, (a, b) in enumerate(PLANES):
        quads.append((k["k4"] * ta[n] + a_rho + (am[a] + am[b]),
                      k["k2"] * hq[n][1],
                      k["k3"] * tc[n][0] + aj[a],
                      k["k3"] * tc[n][1] + aj[b]))
    out = from_pairs(a_rho, [a_rho + v for v in am], aj, quads)
    return out, grad


def here(i):
    return pl.ds(pl.multiple_of(i * ROWS, ROWS), ROWS)


def walkers(ny, nz):
    steps = ny // ROWS

    def shifted(ref, slot, layer, i, sy, sz):
        row = lax.broadcasted_iota(jnp.int32, (ROWS, nz), 0)
        value = ref[slot, layer, pl.ds(pl.multiple_of(i * ROWS, ROWS), ROWS), :]
        if sy:
            near = lax.rem(i + (steps - 1 if sy > 0 else 1), steps)
            other = ref[slot, layer, pl.ds(pl.multiple_of(near * ROWS, ROWS), ROWS), :]
            value = jnp.where(row == (ROWS - 1 if sy > 0 else 0), other, value)
            value = pltpu.roll(value, sy % ROWS, 0)
        if sz:
            value = pltpu.roll(value, sz % nz, 1)
        return value

    def streamed(ref, x, i, sign, slots, without=()):
        return [jnp.zeros((ROWS, nz), jnp.float32) if VEL[q][0] in without else
                shifted(ref, slots[q], x + 1 - sign * VEL[q][0], i, sign * VEL[q][1],
                        sign * VEL[q][2]) for q in range(19)]

    def over(layers, body):
        first, stride, number = layers
        if number == 0:
            return

        def step(t, carry):
            body(first + stride * (t // steps), lax.rem(t, steps))
            return carry

        lax.fori_loop(0, number * steps, step, 0, unroll=UNROLL)

    return shifted, streamed, over


def final_body(streamed, adj, mom, por, wal, out, grad):
    def back_zero(x, i):
        at = here(i)
        h = streamed(adj, x, i, -1, SLOT)
        j = [mom[n, x, at, :] for n in range(3)]
        a, part = backward(h, j, mom[3, x, at, :], por[x, at, :], wal[x, at, :] == 1)
        for q in range(19):
            out[q, x, at, :] = a[q]
        grad[x, at, :] = grad[x, at, :] + part

    return back_zero


def near_far(axis, width):
    even = lax.rem(lax.axis_index(axis), 2) == 0
    return even, jnp.where(even, width - 1, 0), jnp.where(even, 0, width - 1)


def finish(done, part, out_hbm, grad_hbm, sem):
    copies = [pltpu.make_async_copy(done, out_hbm, sem.at[0]),
              pltpu.make_async_copy(part, grad_hbm, sem.at[1])]
    for copy in copies:
        copy.start()
    for copy in copies:
        copy.wait()


def kernel(axis, poro_hbm, step_ref, chk_hbm, seed_hbm, mat_hbm, wall_hbm,
           out, grad, poro_ref, chk, mat, wal, mom, por, seed, post, adj, face, halo,
           load_sem, send_sem, recv_sem):
    width, ny, nz = mat.shape
    shifted, streamed, over = walkers(ny, nz)
    count = lax.axis_size(axis)
    me = lax.axis_index(axis)
    right, left = lax.rem(me + 1, count), lax.rem(me + count - 1, count)
    last = width - 1
    edge = [0, last] if width > 1 else [0]
    inner = max(width - 2, 0)

    barrier = pltpu.get_barrier_semaphore()
    for neighbour in (left, right):
        pl.semaphore_signal(barrier, inc=1, device_id={axis: neighbour}, device_id_type=MESH)

    loads = [pltpu.make_async_copy(mat_hbm, mat, load_sem.at[0]),
             pltpu.make_async_copy(wall_hbm, wal, load_sem.at[1])]
    edge_loads = [pltpu.make_async_copy(chk_hbm.at[:, x], chk.at[:, x], load_sem.at[2 + n])
                  for n, x in enumerate(edge)]
    late = []
    if inner:
        late.append(pltpu.make_async_copy(chk_hbm.at[:, pl.ds(1, inner)], chk.at[:, pl.ds(1, inner)],
                                          load_sem.at[4]))
    seed_load = pltpu.make_async_copy(seed_hbm, seed.at[:, pl.ds(1, width)], load_sem.at[5])
    loads.append(pltpu.make_async_copy(poro_hbm, poro_ref, load_sem.at[6]))
    for copy in loads + edge_loads + late + [seed_load]:
        copy.start()

    def remote(src, dst, number, target):
        return pltpu.make_async_remote_copy(
            src_ref=src, dst_ref=dst, send_sem=send_sem.at[number], recv_sem=recv_sem.at[number],
            device_id={axis: target}, device_id_type=MESH)

    seed_sends = []
    for start, size in ((1, 1), (7, 2), (11, 2)):
        seed_sends.append(remote(seed_hbm.at[pl.ds(start, size), 0],
                                 seed.at[pl.ds(start, size), width + 1], len(seed_sends), left))
    for start, size in ((2, 1), (9, 2), (13, 2)):
        seed_sends.append(remote(seed_hbm.at[pl.ds(start, size), last],
                                 seed.at[pl.ds(start, size), 0], len(seed_sends), right))
    post_up = remote(face.at[0], halo.at[0], 6, right)
    post_down = remote(face.at[1], halo.at[1], 7, left)
    adj_down = remote(adj.at[pl.ds(0, 5), 1], adj.at[pl.ds(0, 5), width + 1], 8, left)
    adj_up = remote(adj.at[pl.ds(5, 5), width], adj.at[pl.ds(5, 5), 0], 9, right)

    bottom, top = (0, 1, 1), (last, 1, 1)
    middle = (1, 1, inner)

    def collide(x, i):
        at = here(i)
        kinds = mat[x, at, :]
        porosity = jnp.zeros((ROWS, nz), jnp.float32)
        for number in range(poro_ref.shape[0]):
            porosity = jnp.where(kinds == number, poro_ref[number], porosity)
        f = [chk[q, x, at, :] for q in range(19)]
        g, j, ratio = forward(f, porosity, wal[x, at, :] == 1, force)
        for q in range(19):
            post[SLOT[q], x + 1, at, :] = g[q]
        por[x, at, :] = porosity
        for n, value in enumerate((*j, ratio)):
            mom[n, x, at, :] = value

    def fold(x, sign):
        def body(_, i):
            moved = {VEL[q][1:]: shifted(post, SLOT[q], x + 1, i, VEL[q][1], VEL[q][2])
                     for q in (PLUS if sign > 0 else MINUS)}
            up, down, fore, aft = moved[1, 0], moved[-1, 0], moved[0, 1], moved[0, -1]
            side = 0 if sign > 0 else 1
            face[side, 0, here(i), :] = moved[0, 0] + (up + down) + (fore + aft)
            face[side, 1, here(i), :] = up - down
            face[side, 2, here(i), :] = fore - aft
        return body

    def back_one(x, i, folded=()):
        at = here(i)
        porosity = por[x, at, :]
        first = streamed(post, x, i, 1, SLOT, [sign for sign, _ in folded])
        density, j = conserved(*to_pairs(first))
        for sign, side in folded:
            total = halo[side, 0, at, :]
            density = density + total
            j = (j[0] + sign * total, j[1] + halo[side, 1, at, :], j[2] + halo[side, 2, at, :])
        h = streamed(seed, x, i, -1, SAME)
        a, part = backward(h, j, porosity / density, porosity, wal[x, at, :] == 1)
        for q in range(19):
            adj[SLOT[q], x + 1, at, :] = a[q]
        grad[x, at, :] = part

    def at_bottom(x, i):
        back_one(x, i, ((1, 0),) if width > 1 else ((1, 0), (-1, 1)))

    def at_top(x, i):
        back_one(x, i, ((-1, 1),))

    back_zero = final_body(streamed, adj, mom, por, wal, out, grad)

    pl.semaphore_wait(barrier, 2)
    for copy in seed_sends:
        copy.start()
    for copy in loads:
        copy.wait()
    turn = (step_ref[0] & 63).astype(jnp.float32) * np.float32(2.0 * np.pi / 64.0)
    force = 0.05 * jnp.sin(jnp.full((ROWS, nz), turn, jnp.float32))
    edge_loads[0].wait()
    over(bottom, collide)
    over(bottom, fold(0, -1))
    post_down.start()
    if width > 1:
        edge_loads[1].wait()
        over(top, collide)
    over(top, fold(last, 1))
    post_up.start()
    for copy in late:
        copy.wait()
    over(middle, collide)
    seed_load.wait()
    over(middle, back_one)
    from_left, from_right = seed_sends[3:] + [post_up], seed_sends[:3] + [post_down]
    for copy in from_left if width > 1 else from_left + from_right:
        copy.wait_recv()
    over(bottom, at_bottom)
    adj_down.start()
    if width > 1:
        for copy in from_right:
            copy.wait_recv()
        over(top, at_top)
    adj_up.start()
    over(middle, back_zero)
    if width > 1:
        even, near, far = near_far(axis, width)

        @pl.when(even)
        def _():
            adj_down.wait_recv()

        @pl.when(jnp.logical_not(even))
        def _():
            adj_up.wait_recv()

        over((near, 1, 1), back_zero)

        @pl.when(even)
        def _():
            adj_up.wait_recv()

        @pl.when(jnp.logical_not(even))
        def _():
            adj_down.wait_recv()

        over((far, 1, 1), back_zero)
    else:
        adj_up.wait_recv()
        adj_down.wait_recv()
        over(bottom, back_zero)
    for copy in seed_sends + [post_up, post_down, adj_up, adj_down]:
        copy.wait_send()


def local(checkpoint, adjoint_seed, material, wall_mask, class_porosity, step_index):
    width, ny, nz = material.shape
    f32 = jnp.float32
    anywhere = pl.BlockSpec(memory_space=pltpu.HBM)
    scalars = pl.BlockSpec(memory_space=pltpu.SMEM)
    vmem = pl.BlockSpec(memory_space=pltpu.VMEM)
    pinned = lambda x: pltpu.with_memory_space_constraint(x, pltpu.HBM)
    cells = (width, ny, nz)
    padded = (19, width + 2, ny, nz)
    shape = jax.ShapeDtypeStruct
    kept = pl.pallas_call(
        functools.partial(kernel, "gx"),
        out_shape=(shape((19,) + cells, f32), shape(cells, f32)),
        in_specs=[anywhere, scalars] + [anywhere] * 4,
        out_specs=(vmem,) * 2,
        scratch_shapes=[
            pltpu.SMEM(class_porosity.shape, f32),
            pltpu.VMEM((19,) + cells, f32),
            pltpu.VMEM(cells, jnp.int32),
            pltpu.VMEM(cells, jnp.int32),
            pltpu.VMEM((4,) + cells, f32),
            pltpu.VMEM(cells, f32),
            pltpu.VMEM(padded, f32),
            pltpu.VMEM(padded, f32),
            pltpu.VMEM(padded, f32),
            pltpu.VMEM((2, 3, ny, nz), f32),
            pltpu.VMEM((2, 3, ny, nz), f32),
            pltpu.SemaphoreType.DMA((7,)),
            pltpu.SemaphoreType.DMA((10,)),
            pltpu.SemaphoreType.DMA((10,)),
        ],
        compiler_params=pltpu.CompilerParams(
            collective_id=0, has_side_effects=True, vmem_limit_bytes=28 * 2**20),
    )(pinned(class_porosity), step_index, pinned(checkpoint), pinned(adjoint_seed),
      pinned(material), pinned(wall_mask))
    return pl.pallas_call(
        finish,
        out_shape=(shape((19,) + cells, f32), shape(cells, f32)),
        in_specs=[vmem] * 2,
        out_specs=(anywhere, anywhere),
        scratch_shapes=[
            pltpu.SemaphoreType.DMA((2,)),
        ],
    )(*kept)


def solution(mesh):
    placed = (
        P(None, "gx", "groups", None),
        P(None, "gx", "groups", None),
        P("gx", "groups", None),
        P("gx", "groups", None),
        P(),
        P("groups"),
    )
    return jax.shard_map(
        local,
        mesh=mesh,
        in_specs=placed,
        out_specs=(P(None, "gx", "groups", None), P("gx", "groups", None)),
        check_vma=False,
    )
```

```python
import functools

import jax
import jax.numpy as jnp
import numpy as np
from jax import lax
from jax.experimental import pallas as pl
from jax.experimental.pallas import tpu as pltpu
from jax.sharding import PartitionSpec as P

MESH = pl.DeviceIdType.MESH
ROWS = 8
UNROLL = 4


def velocity_list():
    rows = [(0, 0, 0)]
    for axis in range(3):
        for sign in (1, -1):
            entry = [0, 0, 0]
            entry[axis] = sign
            rows.append(tuple(entry))
    for first, second in ((0, 1), (0, 2), (1, 2)):
        for one in (1, -1):
            for two in (1, -1):
                entry = [0, 0, 0]
                entry[first] = one
                entry[second] = two
                rows.append(tuple(entry))
    return rows


VEL = velocity_list()
PLUS = [q for q in range(19) if VEL[q][0] == 1]
MINUS = [q for q in range(19) if VEL[q][0] == -1]
REST = [q for q in range(19) if VEL[q][0] == 0]
SLOT = {q: pos for pos, q in enumerate(PLUS + MINUS + REST)}
SAME = {q: q for q in range(19)}
AXIS = [(VEL.index(tuple(int(a == d) for d in range(3))),
         VEL.index(tuple(-int(a == d) for d in range(3)))) for a in range(3)]
PLANES = ((0, 1), (0, 2), (1, 2))


def corner(plane, one, two):
    entry = [0, 0, 0]
    entry[plane[0]] = one
    entry[plane[1]] = two
    return VEL.index(tuple(entry))


def to_pairs(f):
    sums = [f[p] + f[m] for p, m in AXIS]
    diffs = [f[p] - f[m] for p, m in AXIS]
    quads = []
    for plane in PLANES:
        pp, pm = f[corner(plane, 1, 1)], f[corner(plane, 1, -1)]
        mp, mm = f[corner(plane, -1, 1)], f[corner(plane, -1, -1)]
        s1, d1, s2, d2 = pp + pm, pp - pm, mp + mm, mp - mm
        quads.append((s1 + s2, d1 - d2, s1 - s2, d1 + d2))
    return f[0], sums, diffs, quads


def from_pairs(rest, sums, diffs, quads):
    out = {0: rest}
    for a, (p, m) in enumerate(AXIS):
        out[p] = sums[a] + diffs[a]
        out[m] = sums[a] - diffs[a]
    for plane, (qa, qb, qc, qd) in zip(PLANES, quads):
        s1, s2, d1, d2 = qa + qc, qa - qc, qb + qd, qd - qb
        out[corner(plane, 1, 1)] = s1 + d1
        out[corner(plane, 1, -1)] = s1 - d1
        out[corner(plane, -1, 1)] = s2 + d2
        out[corner(plane, -1, -1)] = s2 - d2
    return out


def conserved(rest, sums, diffs, quads):
    axy, axz, ayz = quads[0][0], quads[1][0], quads[2][0]
    density = (rest + (sums[0] + sums[1])) + (sums[2] + axy) + (axz + ayz)
    jx = diffs[0] + (quads[0][2] + quads[1][2])
    jy = diffs[1] + (quads[0][3] + quads[2][2])
    jz = diffs[2] + (quads[1][3] + quads[2][3])
    return density, (jx, jy, jz)


def rates(wall):
    pick = lambda at_wall, inside: jnp.where(wall, jnp.float32(at_wall), jnp.float32(inside))
    return dict(k2=pick(1, -0.6), s2=pick(0, 1.6), k3=pick(-1, -0.4), s3=pick(0, 1.4 / 3.0),
                k4=pick(1, -0.2), s4=pick(0, 1.2), sg=pick(-1, 1))


def forward(f, porosity, wall, force):
    k = rates(wall)
    rest, sums, diffs, quads = to_pairs(f)
    density, j = conserved(rest, sums, diffs, quads)
    ratio = porosity / density
    q = [porosity * c for c in j]
    u = [ratio * c for c in j]
    pxx, pyy, pzz = [q[a] * u[a] for a in range(3)]
    push = jnp.where(wall, 0.0, force)
    push3 = push * (1.0 / 3.0)
    third = density * (1.0 / 3.0)
    ninth = density * (1.0 / 9.0)
    a_of = [quads[n][0] for n in range(3)]
    even = [ninth + (pxx + pyy) * (1.0 / 3.0) - pzz * (1.0 / 6.0),
            ninth + (pxx + pzz) * (1.0 / 3.0) - pyy * (1.0 / 6.0),
            ninth + (pyy + pzz) * (1.0 / 3.0) - pxx * (1.0 / 6.0)]
    m = [sums[0] + (a_of[0] + a_of[1]), sums[1] + (a_of[0] + a_of[2]), sums[2] + (a_of[1] + a_of[2])]
    ms = [k["k2"] * m[a] + k["s2"] * (third + p) for a, p in enumerate((pxx, pyy, pzz))]
    new = []
    odd = [k["s3"] * q[0] + push3, k["s3"] * q[1], k["s3"] * q[2]]
    for n, (a, b) in enumerate(PLANES):
        qa, qb, qc, qd = quads[n]
        new.append((k["k4"] * qa + k["s4"] * even[n],
                    k["k2"] * qb + k["s2"] * (q[a] * u[b]),
                    k["k3"] * qc + odd[a],
                    k["k3"] * qd + odd[b]))
    axy, axz, ayz = new[0][0], new[1][0], new[2][0]
    s_new = [ms[0] - (axy + axz), ms[1] - (axy + ayz), ms[2] - (axz + ayz)]
    d_new = [(k["sg"] * j[0] + push) - (new[0][2] + new[1][2]),
             k["sg"] * j[1] - (new[0][3] + new[2][2]),
             k["sg"] * j[2] - (new[1][3] + new[2][3])]
    rest_new = density - (ms[0] + ms[1] + ms[2]) + (axy + axz + ayz)
    out = from_pairs(rest_new, [0.5 * s for s in s_new], [0.5 * d for d in d_new],
                     [tuple(0.25 * v for v in quad) for quad in new])
    return out, j, ratio


def backward(h, j, ratio, porosity, wall):
    k = rates(wall)
    h0, hs, hd, hq = to_pairs(h)
    hs = [0.5 * v for v in hs]
    hd = [0.5 * v for v in hd]
    hq = [tuple(0.25 * v for v in quad) for quad in hq]
    u = [ratio * c for c in j]
    ts = [v - h0 for v in hs]
    ta = [hq[n][0] - h0 - (ts[a] + ts[b]) for n, (a, b) in enumerate(PLANES)]
    tc = [(hq[n][2] - hd[a], hq[n][3] - hd[b]) for n, (a, b) in enumerate(PLANES)]
    ea = [k["s4"] * v for v in ta]
    eb = [k["s2"] * quad[1] for quad in hq]
    em = [k["s2"] * v for v in ts]
    px = em[0] + (ea[0] + ea[1]) * (1.0 / 3.0) - ea[2] * (1.0 / 6.0)
    py = em[1] + (ea[0] + ea[2]) * (1.0 / 3.0) - ea[1] * (1.0 / 6.0)
    pz = em[2] + (ea[1] + ea[2]) * (1.0 / 3.0) - ea[0] * (1.0 / 6.0)
    gx = 2.0 * px * u[0] + (eb[0] * u[1] + eb[1] * u[2])
    gy = 2.0 * py * u[1] + (eb[0] * u[0] + eb[2] * u[2])
    gz = 2.0 * pz * u[2] + (eb[1] * u[0] + eb[2] * u[1])
    a_rho = (h0 + (em[0] + em[1] + em[2]) * (1.0 / 3.0) + (ea[0] + ea[1] + ea[2]) * (1.0 / 9.0)
             - 0.5 * (u[0] * gx + u[1] * gy + u[2] * gz))
    g = [gx + k["s3"] * (tc[0][0] + tc[1][0]),
         gy + k["s3"] * (tc[0][1] + tc[2][0]),
         gz + k["s3"] * (tc[1][1] + tc[2][1])]
    grad = j[0] * g[0] + j[1] * g[1] + j[2] * g[2]
    aj = [k["sg"] * hd[a] + porosity * g[a] for a in range(3)]
    am = [k["k2"] * v for v in ts]
    quads = []
    for n, (a, b) in enumerate(PLANES):
        quads.append((k["k4"] * ta[n] + a_rho + (am[a] + am[b]),
                      k["k2"] * hq[n][1],
                      k["k3"] * tc[n][0] + aj[a],
                      k["k3"] * tc[n][1] + aj[b]))
    out = from_pairs(a_rho, [a_rho + v for v in am], aj, quads)
    return out, grad


def here(i):
    return pl.ds(pl.multiple_of(i * ROWS, ROWS), ROWS)


def walkers(ny, nz):
    steps = ny // ROWS

    def shifted(ref, slot, layer, i, sy, sz):
        row = lax.broadcasted_iota(jnp.int32, (ROWS, nz), 0)
        value = ref[slot, layer, pl.ds(pl.multiple_of(i * ROWS, ROWS), ROWS), :]
        if sy:
            near = lax.rem(i + (steps - 1 if sy > 0 else 1), steps)
            other = ref[slot, layer, pl.ds(pl.multiple_of(near * ROWS, ROWS), ROWS), :]
            value = jnp.where(row == (ROWS - 1 if sy > 0 else 0), other, value)
            value = pltpu.roll(value, sy % ROWS, 0)
        if sz:
            value = pltpu.roll(value, sz % nz, 1)
        return value

    def streamed(ref, x, i, sign, slots, without=()):
        return [jnp.zeros((ROWS, nz), jnp.float32) if VEL[q][0] in without else
                shifted(ref, slots[q], x + 1 - sign * VEL[q][0], i, sign * VEL[q][1],
                        sign * VEL[q][2]) for q in range(19)]

    def over(layers, body):
        first, stride, number = layers
        if number == 0:
            return

        def step(t, carry):
            body(first + stride * (t // steps), lax.rem(t, steps))
            return carry

        lax.fori_loop(0, number * steps, step, 0, unroll=UNROLL)

    return shifted, streamed, over


def final_body(streamed, adj, mom, por, wal, out, grad):
    def back_zero(x, i):
        at = here(i)
        h = streamed(adj, x, i, -1, SLOT)
        j = [mom[n, x, at, :] for n in range(3)]
        a, part = backward(h, j, mom[3, x, at, :], por[x, at, :], wal[x, at, :] == 1)
        for q in range(19):
            out[q, x, at, :] = a[q]
        grad[x, at, :] = grad[x, at, :] + part

    return back_zero


def near_far(axis, width):
    even = lax.rem(lax.axis_index(axis), 2) == 0
    return even, jnp.where(even, width - 1, 0), jnp.where(even, 0, width - 1)


def finish(done, part, out_hbm, grad_hbm, sem):
    copies = [pltpu.make_async_copy(done.at[pl.ds(q, min(5, 19 - q))],
                                    out_hbm.at[pl.ds(q, min(5, 19 - q))], sem.at[q // 5])
              for q in range(0, 19, 5)]
    copies.append(pltpu.make_async_copy(part, grad_hbm, sem.at[4]))
    for copy in copies:
        copy.start()
    for copy in copies:
        copy.wait()


def kernel(axis, poro_hbm, step_ref, chk_hbm, seed_hbm, mat_hbm, wall_hbm,
           out, grad, poro_ref, chk, mat, wal, mom, por, seed, post, adj, face, halo,
           load_sem, send_sem, recv_sem):
    width, ny, nz = mat.shape
    shifted, streamed, over = walkers(ny, nz)
    count = lax.axis_size(axis)
    me = lax.axis_index(axis)
    right, left = lax.rem(me + 1, count), lax.rem(me + count - 1, count)
    last = width - 1
    edge = [0, last] if width > 1 else [0]
    inner = max(width - 2, 0)

    barrier = pltpu.get_barrier_semaphore()
    for neighbour in (left, right):
        pl.semaphore_signal(barrier, inc=1, device_id={axis: neighbour}, device_id_type=MESH)

    loads = [pltpu.make_async_copy(mat_hbm, mat, load_sem.at[0]),
             pltpu.make_async_copy(wall_hbm, wal, load_sem.at[1])]
    edge_loads = [pltpu.make_async_copy(chk_hbm.at[:, x], chk.at[:, x], load_sem.at[2 + n])
                  for n, x in enumerate(edge)]
    late = []
    if inner:
        late.append(pltpu.make_async_copy(chk_hbm.at[:, pl.ds(1, inner)], chk.at[:, pl.ds(1, inner)],
                                          load_sem.at[4]))
    seed_load = pltpu.make_async_copy(seed_hbm, seed.at[:, pl.ds(1, width)], load_sem.at[5])
    loads.append(pltpu.make_async_copy(poro_hbm, poro_ref, load_sem.at[6]))
    for copy in loads + edge_loads + late + [seed_load]:
        copy.start()

    def remote(src, dst, number, target):
        return pltpu.make_async_remote_copy(
            src_ref=src, dst_ref=dst, send_sem=send_sem.at[number], recv_sem=recv_sem.at[number],
            device_id={axis: target}, device_id_type=MESH)

    seed_sends = []
    for start, size in ((1, 1), (7, 2), (11, 2)):
        seed_sends.append(remote(seed_hbm.at[pl.ds(start, size), 0],
                                 seed.at[pl.ds(start, size), width + 1], len(seed_sends), left))
    for start, size in ((2, 1), (9, 2), (13, 2)):
        seed_sends.append(remote(seed_hbm.at[pl.ds(start, size), last],
                                 seed.at[pl.ds(start, size), 0], len(seed_sends), right))
    post_up = remote(face.at[0], halo.at[0], 6, right)
    post_down = remote(face.at[1], halo.at[1], 7, left)
    adj_down = remote(adj.at[pl.ds(0, 5), 1], adj.at[pl.ds(0, 5), width + 1], 8, left)
    adj_up = remote(adj.at[pl.ds(5, 5), width], adj.at[pl.ds(5, 5), 0], 9, right)

    bottom, top = (0, 1, 1), (last, 1, 1)
    middle = (1, 1, inner)

    def collide(x, i):
        at = here(i)
        kinds = mat[x, at, :]
        porosity = jnp.zeros((ROWS, nz), jnp.float32)
        for number in range(poro_ref.shape[0]):
            porosity = jnp.where(kinds == number, poro_ref[number], porosity)
        f = [chk[q, x, at, :] for q in range(19)]
        g, j, ratio = forward(f, porosity, wal[x, at, :] == 1, force)
        for q in range(19):
            post[SLOT[q], x + 1, at, :] = g[q]
        por[x, at, :] = porosity
        for n, value in enumerate((*j, ratio)):
            mom[n, x, at, :] = value

    def fold(x, sign):
        def body(_, i):
            moved = {VEL[q][1:]: shifted(post, SLOT[q], x + 1, i, VEL[q][1], VEL[q][2])
                     for q in (PLUS if sign > 0 else MINUS)}
            up, down, fore, aft = moved[1, 0], moved[-1, 0], moved[0, 1], moved[0, -1]
            side = 0 if sign > 0 else 1
            face[side, 0, here(i), :] = moved[0, 0] + (up + down) + (fore + aft)
            face[side, 1, here(i), :] = up - down
            face[side, 2, here(i), :] = fore - aft
        return body

    def back_one(x, i, folded=()):
        at = here(i)
        porosity = por[x, at, :]
        first = streamed(post, x, i, 1, SLOT, [sign for sign, _ in folded])
        density, j = conserved(*to_pairs(first))
        for sign, side in folded:
            total = halo[side, 0, at, :]
            density = density + total
            j = (j[0] + sign * total, j[1] + halo[side, 1, at, :], j[2] + halo[side, 2, at, :])
        h = streamed(seed, x, i, -1, SAME)
        a, part = backward(h, j, porosity / density, porosity, wal[x, at, :] == 1)
        for q in range(19):
            adj[SLOT[q], x + 1, at, :] = a[q]
        grad[x, at, :] = part

    def at_bottom(x, i):
        back_one(x, i, ((1, 0),) if width > 1 else ((1, 0), (-1, 1)))

    def at_top(x, i):
        back_one(x, i, ((-1, 1),))

    back_zero = final_body(streamed, adj, mom, por, wal, out, grad)

    pl.semaphore_wait(barrier, 2)
    for copy in seed_sends:
        copy.start()
    for copy in loads:
        copy.wait()
    turn = (step_ref[0] & 63).astype(jnp.float32) * np.float32(2.0 * np.pi / 64.0)
    force = 0.05 * jnp.sin(jnp.full((ROWS, nz), turn, jnp.float32))
    edge_loads[0].wait()
    over(bottom, collide)
    over(bottom, fold(0, -1))
    post_down.start()
    if width > 1:
        edge_loads[1].wait()
        over(top, collide)
    over(top, fold(last, 1))
    post_up.start()
    for copy in late:
        copy.wait()
    over(middle, collide)
    seed_load.wait()
    over(middle, back_one)
    from_left, from_right = seed_sends[3:] + [post_up], seed_sends[:3] + [post_down]
    for copy in from_left if width > 1 else from_left + from_right:
        copy.wait_recv()
    over(bottom, at_bottom)
    adj_down.start()
    if width > 1:
        for copy in from_right:
            copy.wait_recv()
        over(top, at_top)
    adj_up.start()
    over(middle, back_zero)
    if width > 1:
        even, near, far = near_far(axis, width)

        @pl.when(even)
        def _():
            adj_down.wait_recv()

        @pl.when(jnp.logical_not(even))
        def _():
            adj_up.wait_recv()

        over((near, 1, 1), back_zero)

        @pl.when(even)
        def _():
            adj_up.wait_recv()

        @pl.when(jnp.logical_not(even))
        def _():
            adj_down.wait_recv()

        over((far, 1, 1), back_zero)
    else:
        adj_up.wait_recv()
        adj_down.wait_recv()
        over(bottom, back_zero)
    for copy in seed_sends + [post_up, post_down, adj_up, adj_down]:
        copy.wait_send()


def local(checkpoint, adjoint_seed, material, wall_mask, class_porosity, step_index):
    width, ny, nz = material.shape
    f32 = jnp.float32
    anywhere = pl.BlockSpec(memory_space=pltpu.HBM)
    scalars = pl.BlockSpec(memory_space=pltpu.SMEM)
    vmem = pl.BlockSpec(memory_space=pltpu.VMEM)
    pinned = lambda x: pltpu.with_memory_space_constraint(x, pltpu.HBM)
    cells = (width, ny, nz)
    padded = (19, width + 2, ny, nz)
    shape = jax.ShapeDtypeStruct
    kept = pl.pallas_call(
        functools.partial(kernel, "gx"),
        out_shape=(shape((19,) + cells, f32), shape(cells, f32)),
        in_specs=[anywhere, scalars] + [anywhere] * 4,
        out_specs=(vmem,) * 2,
        scratch_shapes=[
            pltpu.SMEM(class_porosity.shape, f32),
            pltpu.VMEM((19,) + cells, f32),
            pltpu.VMEM(cells, jnp.int32),
            pltpu.VMEM(cells, jnp.int32),
            pltpu.VMEM((4,) + cells, f32),
            pltpu.VMEM(cells, f32),
            pltpu.VMEM(padded, f32),
            pltpu.VMEM(padded, f32),
            pltpu.VMEM(padded, f32),
            pltpu.VMEM((2, 3, ny, nz), f32),
            pltpu.VMEM((2, 3, ny, nz), f32),
            pltpu.SemaphoreType.DMA((7,)),
            pltpu.SemaphoreType.DMA((10,)),
            pltpu.SemaphoreType.DMA((10,)),
        ],
        compiler_params=pltpu.CompilerParams(
            collective_id=0, has_side_effects=True, vmem_limit_bytes=28 * 2**20),
    )(pinned(class_porosity), step_index, pinned(checkpoint), pinned(adjoint_seed),
      pinned(material), pinned(wall_mask))
    return pl.pallas_call(
        finish,
        out_shape=(shape((19,) + cells, f32), shape(cells, f32)),
        in_specs=[vmem] * 2,
        out_specs=(anywhere, anywhere),
        scratch_shapes=[
            pltpu.SemaphoreType.DMA((5,)),
        ],
        compiler_params=pltpu.CompilerParams(vmem_limit_bytes=8 * 2**20),
    )(*kept)


def solution(mesh):
    placed = (
        P(None, "gx", "groups", None),
        P(None, "gx", "groups", None),
        P("gx", "groups", None),
        P("gx", "groups", None),
        P(),
        P("groups"),
    )
    return jax.shard_map(
        local,
        mesh=mesh,
        in_specs=placed,
        out_specs=(P(None, "gx", "groups", None), P("gx", "groups", None)),
        check_vma=False,
    )
```

```python
import functools

import jax
import jax.numpy as jnp
import numpy as np
from jax import lax
from jax.experimental import pallas as pl
from jax.experimental.pallas import tpu as pltpu
from jax.sharding import PartitionSpec as P

MESH = pl.DeviceIdType.MESH
ROWS = 8
UNROLL = 4


def velocity_list():
    rows = [(0, 0, 0)]
    for axis in range(3):
        for sign in (1, -1):
            entry = [0, 0, 0]
            entry[axis] = sign
            rows.append(tuple(entry))
    for first, second in ((0, 1), (0, 2), (1, 2)):
        for one in (1, -1):
            for two in (1, -1):
                entry = [0, 0, 0]
                entry[first] = one
                entry[second] = two
                rows.append(tuple(entry))
    return rows


VEL = velocity_list()
PLUS = [q for q in range(19) if VEL[q][0] == 1]
MINUS = [q for q in range(19) if VEL[q][0] == -1]
REST = [q for q in range(19) if VEL[q][0] == 0]
SLOT = {q: pos for pos, q in enumerate(PLUS + MINUS + REST)}
SAME = {q: q for q in range(19)}
AXIS = [(VEL.index(tuple(int(a == d) for d in range(3))),
         VEL.index(tuple(-int(a == d) for d in range(3)))) for a in range(3)]
PLANES = ((0, 1), (0, 2), (1, 2))


def corner(plane, one, two):
    entry = [0, 0, 0]
    entry[plane[0]] = one
    entry[plane[1]] = two
    return VEL.index(tuple(entry))


def to_pairs(f):
    sums = [f[p] + f[m] for p, m in AXIS]
    diffs = [f[p] - f[m] for p, m in AXIS]
    quads = []
    for plane in PLANES:
        pp, pm = f[corner(plane, 1, 1)], f[corner(plane, 1, -1)]
        mp, mm = f[corner(plane, -1, 1)], f[corner(plane, -1, -1)]
        s1, d1, s2, d2 = pp + pm, pp - pm, mp + mm, mp - mm
        quads.append((s1 + s2, d1 - d2, s1 - s2, d1 + d2))
    return f[0], sums, diffs, quads


def from_pairs(rest, sums, diffs, quads):
    out = {0: rest}
    for a, (p, m) in enumerate(AXIS):
        out[p] = sums[a] + diffs[a]
        out[m] = sums[a] - diffs[a]
    for plane, (qa, qb, qc, qd) in zip(PLANES, quads):
        s1, s2, d1, d2 = qa + qc, qa - qc, qb + qd, qd - qb
        out[corner(plane, 1, 1)] = s1 + d1
        out[corner(plane, 1, -1)] = s1 - d1
        out[corner(plane, -1, 1)] = s2 + d2
        out[corner(plane, -1, -1)] = s2 - d2
    return out


def conserved(rest, sums, diffs, quads):
    axy, axz, ayz = quads[0][0], quads[1][0], quads[2][0]
    density = (rest + (sums[0] + sums[1])) + (sums[2] + axy) + (axz + ayz)
    jx = diffs[0] + (quads[0][2] + quads[1][2])
    jy = diffs[1] + (quads[0][3] + quads[2][2])
    jz = diffs[2] + (quads[1][3] + quads[2][3])
    return density, (jx, jy, jz)


def rates(wall):
    pick = lambda at_wall, inside: jnp.where(wall, jnp.float32(at_wall), jnp.float32(inside))
    return dict(k2=pick(1, -0.6), s2=pick(0, 1.6), k3=pick(-1, -0.4), s3=pick(0, 1.4 / 3.0),
                k4=pick(1, -0.2), s4=pick(0, 1.2), sg=pick(-1, 1))


def forward(f, porosity, wall, force):
    k = rates(wall)
    rest, sums, diffs, quads = to_pairs(f)
    density, j = conserved(rest, sums, diffs, quads)
    ratio = porosity / density
    q = [porosity * c for c in j]
    u = [ratio * c for c in j]
    pxx, pyy, pzz = [q[a] * u[a] for a in range(3)]
    push = jnp.where(wall, 0.0, force)
    push3 = push * (1.0 / 3.0)
    third = density * (1.0 / 3.0)
    ninth = density * (1.0 / 9.0)
    a_of = [quads[n][0] for n in range(3)]
    even = [ninth + (pxx + pyy) * (1.0 / 3.0) - pzz * (1.0 / 6.0),
            ninth + (pxx + pzz) * (1.0 / 3.0) - pyy * (1.0 / 6.0),
            ninth + (pyy + pzz) * (1.0 / 3.0) - pxx * (1.0 / 6.0)]
    m = [sums[0] + (a_of[0] + a_of[1]), sums[1] + (a_of[0] + a_of[2]), sums[2] + (a_of[1] + a_of[2])]
    ms = [k["k2"] * m[a] + k["s2"] * (third + p) for a, p in enumerate((pxx, pyy, pzz))]
    new = []
    odd = [k["s3"] * q[0] + push3, k["s3"] * q[1], k["s3"] * q[2]]
    for n, (a, b) in enumerate(PLANES):
        qa, qb, qc, qd = quads[n]
        new.append((k["k4"] * qa + k["s4"] * even[n],
                    k["k2"] * qb + k["s2"] * (q[a] * u[b]),
                    k["k3"] * qc + odd[a],
                    k["k3"] * qd + odd[b]))
    axy, axz, ayz = new[0][0], new[1][0], new[2][0]
    s_new = [ms[0] - (axy + axz), ms[1] - (axy + ayz), ms[2] - (axz + ayz)]
    d_new = [(k["sg"] * j[0] + push) - (new[0][2] + new[1][2]),
             k["sg"] * j[1] - (new[0][3] + new[2][2]),
             k["sg"] * j[2] - (new[1][3] + new[2][3])]
    rest_new = density - (ms[0] + ms[1] + ms[2]) + (axy + axz + ayz)
    out = from_pairs(rest_new, [0.5 * s for s in s_new], [0.5 * d for d in d_new],
                     [tuple(0.25 * v for v in quad) for quad in new])
    return out, j, ratio


def backward(h, j, ratio, porosity, wall):
    k = rates(wall)
    h0, hs, hd, hq = to_pairs(h)
    hs = [0.5 * v for v in hs]
    hd = [0.5 * v for v in hd]
    hq = [tuple(0.25 * v for v in quad) for quad in hq]
    u = [ratio * c for c in j]
    ts = [v - h0 for v in hs]
    ta = [hq[n][0] - h0 - (ts[a] + ts[b]) for n, (a, b) in enumerate(PLANES)]
    tc = [(hq[n][2] - hd[a], hq[n][3] - hd[b]) for n, (a, b) in enumerate(PLANES)]
    ea = [k["s4"] * v for v in ta]
    eb = [k["s2"] * quad[1] for quad in hq]
    em = [k["s2"] * v for v in ts]
    px = em[0] + (ea[0] + ea[1]) * (1.0 / 3.0) - ea[2] * (1.0 / 6.0)
    py = em[1] + (ea[0] + ea[2]) * (1.0 / 3.0) - ea[1] * (1.0 / 6.0)
    pz = em[2] + (ea[1] + ea[2]) * (1.0 / 3.0) - ea[0] * (1.0 / 6.0)
    gx = 2.0 * px * u[0] + (eb[0] * u[1] + eb[1] * u[2])
    gy = 2.0 * py * u[1] + (eb[0] * u[0] + eb[2] * u[2])
    gz = 2.0 * pz * u[2] + (eb[1] * u[0] + eb[2] * u[1])
    a_rho = (h0 + (em[0] + em[1] + em[2]) * (1.0 / 3.0) + (ea[0] + ea[1] + ea[2]) * (1.0 / 9.0)
             - 0.5 * (u[0] * gx + u[1] * gy + u[2] * gz))
    g = [gx + k["s3"] * (tc[0][0] + tc[1][0]),
         gy + k["s3"] * (tc[0][1] + tc[2][0]),
         gz + k["s3"] * (tc[1][1] + tc[2][1])]
    grad = j[0] * g[0] + j[1] * g[1] + j[2] * g[2]
    aj = [k["sg"] * hd[a] + porosity * g[a] for a in range(3)]
    am = [k["k2"] * v for v in ts]
    quads = []
    for n, (a, b) in enumerate(PLANES):
        quads.append((k["k4"] * ta[n] + a_rho + (am[a] + am[b]),
                      k["k2"] * hq[n][1],
                      k["k3"] * tc[n][0] + aj[a],
                      k["k3"] * tc[n][1] + aj[b]))
    out = from_pairs(a_rho, [a_rho + v for v in am], aj, quads)
    return out, grad


def here(i):
    return pl.ds(pl.multiple_of(i * ROWS, ROWS), ROWS)


def walkers(ny, nz):
    steps = ny // ROWS

    def shifted(ref, slot, layer, i, sy, sz):
        row = lax.broadcasted_iota(jnp.int32, (ROWS, nz), 0)
        value = ref[slot, layer, pl.ds(pl.multiple_of(i * ROWS, ROWS), ROWS), :]
        if sy:
            near = lax.rem(i + (steps - 1 if sy > 0 else 1), steps)
            other = ref[slot, layer, pl.ds(pl.multiple_of(near * ROWS, ROWS), ROWS), :]
            value = jnp.where(row == (ROWS - 1 if sy > 0 else 0), other, value)
            value = pltpu.roll(value, sy % ROWS, 0)
        if sz:
            value = pltpu.roll(value, sz % nz, 1)
        return value

    def streamed(ref, x, i, sign, slots, without=()):
        return [jnp.zeros((ROWS, nz), jnp.float32) if VEL[q][0] in without else
                shifted(ref, slots[q], x + 1 - sign * VEL[q][0], i, sign * VEL[q][1],
                        sign * VEL[q][2]) for q in range(19)]

    def over(layers, body):
        first, stride, number = layers
        if number == 0:
            return

        def step(t, carry):
            body(first + stride * (t // steps), lax.rem(t, steps))
            return carry

        lax.fori_loop(0, number * steps, step, 0, unroll=UNROLL)

    return shifted, streamed, over


def final_body(streamed, adj, mom, por, wal, out, grad):
    def back_zero(x, i):
        at = here(i)
        h = streamed(adj, x, i, -1, SLOT)
        j = [mom[n, x, at, :] for n in range(3)]
        a, part = backward(h, j, mom[3, x, at, :], por[x, at, :], wal[x, at, :] == 1)
        for q in range(19):
            out[q, x, at, :] = a[q]
        grad[x, at, :] = grad[x, at, :] + part

    return back_zero


def near_far(axis, width):
    even = lax.rem(lax.axis_index(axis), 2) == 0
    return even, jnp.where(even, width - 1, 0), jnp.where(even, 0, width - 1)


def finish(done, part, out_hbm, grad_hbm, sem):
    copies = [pltpu.make_async_copy(done.at[pl.ds(q, min(5, 19 - q))],
                                    out_hbm.at[pl.ds(q, min(5, 19 - q))], sem.at[q // 5])
              for q in range(0, 19, 5)]
    copies.append(pltpu.make_async_copy(part, grad_hbm, sem.at[4]))
    for copy in copies:
        copy.start()
    for copy in copies:
        copy.wait()


def kernel(axis, poro_hbm, step_ref, chk_hbm, seed_hbm, mat_hbm, wall_hbm,
           out, grad, poro_ref, chk, mat, wal, mom, por, seed, post, adj, face, halo,
           load_sem, send_sem, recv_sem):
    width, ny, nz = mat.shape
    shifted, streamed, over = walkers(ny, nz)
    count = lax.axis_size(axis)
    me = lax.axis_index(axis)
    right, left = lax.rem(me + 1, count), lax.rem(me + count - 1, count)
    last = width - 1
    edge = [0, last] if width > 1 else [0]
    inner = max(width - 2, 0)

    barrier = pltpu.get_barrier_semaphore()
    for neighbour in (left, right):
        pl.semaphore_signal(barrier, inc=1, device_id={axis: neighbour}, device_id_type=MESH)

    loads = [pltpu.make_async_copy(mat_hbm, mat, load_sem.at[0]),
             pltpu.make_async_copy(wall_hbm, wal, load_sem.at[1])]
    edge_loads = [pltpu.make_async_copy(chk_hbm.at[:, x], chk.at[:, x], load_sem.at[2 + n])
                  for n, x in enumerate(edge)]
    late = []
    if inner:
        late.append(pltpu.make_async_copy(chk_hbm.at[:, pl.ds(1, inner)], chk.at[:, pl.ds(1, inner)],
                                          load_sem.at[4]))
    seed_load = pltpu.make_async_copy(seed_hbm, seed.at[:, pl.ds(1, width)], load_sem.at[5])
    loads.append(pltpu.make_async_copy(poro_hbm, poro_ref, load_sem.at[6]))
    for copy in loads + edge_loads + late + [seed_load]:
        copy.start()

    def remote(src, dst, number, target):
        return pltpu.make_async_remote_copy(
            src_ref=src, dst_ref=dst, send_sem=send_sem.at[number], recv_sem=recv_sem.at[number],
            device_id={axis: target}, device_id_type=MESH)

    seed_sends = []
    for start, size in ((1, 1), (7, 2), (11, 2)):
        seed_sends.append(remote(seed_hbm.at[pl.ds(start, size), 0],
                                 seed.at[pl.ds(start, size), width + 1], len(seed_sends), left))
    for start, size in ((2, 1), (9, 2), (13, 2)):
        seed_sends.append(remote(seed_hbm.at[pl.ds(start, size), last],
                                 seed.at[pl.ds(start, size), 0], len(seed_sends), right))
    post_up = remote(face.at[0], halo.at[0], 6, right)
    post_down = remote(face.at[1], halo.at[1], 7, left)
    adj_down = remote(adj.at[pl.ds(0, 5), 1], adj.at[pl.ds(0, 5), width + 1], 8, left)
    adj_up = remote(adj.at[pl.ds(5, 5), width], adj.at[pl.ds(5, 5), 0], 9, right)

    bottom, top = (0, 1, 1), (last, 1, 1)
    middle = (1, 1, inner)

    def collide(x, i):
        at = here(i)
        kinds = mat[x, at, :]
        porosity = jnp.zeros((ROWS, nz), jnp.float32)
        for number in range(poro_ref.shape[0]):
            porosity = jnp.where(kinds == number, poro_ref[number], porosity)
        f = [chk[q, x, at, :] for q in range(19)]
        g, j, ratio = forward(f, porosity, wal[x, at, :] == 1, force)
        for q in range(19):
            post[SLOT[q], x + 1, at, :] = g[q]
        por[x, at, :] = porosity
        for n, value in enumerate((*j, ratio)):
            mom[n, x, at, :] = value

    def fold(x, sign):
        def body(_, i):
            moved = {VEL[q][1:]: shifted(post, SLOT[q], x + 1, i, VEL[q][1], VEL[q][2])
                     for q in (PLUS if sign > 0 else MINUS)}
            up, down, fore, aft = moved[1, 0], moved[-1, 0], moved[0, 1], moved[0, -1]
            side = 0 if sign > 0 else 1
            face[side, 0, here(i), :] = moved[0, 0] + (up + down) + (fore + aft)
            face[side, 1, here(i), :] = up - down
            face[side, 2, here(i), :] = fore - aft
        return body

    def back_one(x, i, folded=()):
        at = here(i)
        porosity = por[x, at, :]
        first = streamed(post, x, i, 1, SLOT, [sign for sign, _ in folded])
        density, j = conserved(*to_pairs(first))
        for sign, side in folded:
            total = halo[side, 0, at, :]
            density = density + total
            j = (j[0] + sign * total, j[1] + halo[side, 1, at, :], j[2] + halo[side, 2, at, :])
        h = streamed(seed, x, i, -1, SAME)
        a, part = backward(h, j, porosity / density, porosity, wal[x, at, :] == 1)
        for q in range(19):
            adj[SLOT[q], x + 1, at, :] = a[q]
        grad[x, at, :] = part

    def at_bottom(x, i):
        back_one(x, i, ((1, 0),) if width > 1 else ((1, 0), (-1, 1)))

    def at_top(x, i):
        back_one(x, i, ((-1, 1),))

    back_zero = final_body(streamed, adj, mom, por, wal, out, grad)

    turn = (step_ref[0] & 63).astype(jnp.float32) * np.float32(2.0 * np.pi / 64.0)
    force = 0.05 * jnp.sin(jnp.full((ROWS, nz), turn, jnp.float32))
    even, near, far = near_far(axis, width)

    def by_side(first, second):
        @pl.when(even)
        def _():
            first()

        second()

        @pl.when(jnp.logical_not(even))
        def _():
            first()

    def send_seeds(group):
        for copy in group:
            copy.start()

    def send_bottom():
        over(bottom, fold(0, -1))
        post_down.start()

    def send_top():
        over(top, fold(last, 1))
        post_up.start()

    pl.semaphore_wait(barrier, 2)
    by_side(lambda: send_seeds(seed_sends[:3]), lambda: send_seeds(seed_sends[3:]))
    for copy in loads + edge_loads:
        copy.wait()
    if width > 1:
        over((far, 1, 1), collide)

        @pl.when(even)
        def _():
            send_bottom()

        @pl.when(jnp.logical_not(even))
        def _():
            send_top()

        over((near, 1, 1), collide)

        @pl.when(even)
        def _():
            send_top()

        @pl.when(jnp.logical_not(even))
        def _():
            send_bottom()
    else:
        over(bottom, collide)
        send_bottom()
        send_top()
    for copy in late:
        copy.wait()
    over(middle, collide)
    seed_load.wait()
    over(middle, back_one)
    from_left, from_right = seed_sends[3:] + [post_up], seed_sends[:3] + [post_down]
    for copy in from_left if width > 1 else from_left + from_right:
        copy.wait_recv()
    over(bottom, at_bottom)
    adj_down.start()
    if width > 1:
        for copy in from_right:
            copy.wait_recv()
        over(top, at_top)
    adj_up.start()
    over(middle, back_zero)
    if width > 1:
        @pl.when(even)
        def _():
            adj_down.wait_recv()

        @pl.when(jnp.logical_not(even))
        def _():
            adj_up.wait_recv()

        over((near, 1, 1), back_zero)

        @pl.when(even)
        def _():
            adj_up.wait_recv()

        @pl.when(jnp.logical_not(even))
        def _():
            adj_down.wait_recv()

        over((far, 1, 1), back_zero)
    else:
        adj_up.wait_recv()
        adj_down.wait_recv()
        over(bottom, back_zero)
    for copy in seed_sends + [post_up, post_down, adj_up, adj_down]:
        copy.wait_send()


def local(checkpoint, adjoint_seed, material, wall_mask, class_porosity, step_index):
    width, ny, nz = material.shape
    f32 = jnp.float32
    anywhere = pl.BlockSpec(memory_space=pltpu.HBM)
    scalars = pl.BlockSpec(memory_space=pltpu.SMEM)
    vmem = pl.BlockSpec(memory_space=pltpu.VMEM)
    pinned = lambda x: pltpu.with_memory_space_constraint(x, pltpu.HBM)
    cells = (width, ny, nz)
    padded = (19, width + 2, ny, nz)
    shape = jax.ShapeDtypeStruct
    kept = pl.pallas_call(
        functools.partial(kernel, "gx"),
        out_shape=(shape((19,) + cells, f32), shape(cells, f32)),
        in_specs=[anywhere, scalars] + [anywhere] * 4,
        out_specs=(vmem,) * 2,
        scratch_shapes=[
            pltpu.SMEM(class_porosity.shape, f32),
            pltpu.VMEM((19,) + cells, f32),
            pltpu.VMEM(cells, jnp.int32),
            pltpu.VMEM(cells, jnp.int32),
            pltpu.VMEM((4,) + cells, f32),
            pltpu.VMEM(cells, f32),
            pltpu.VMEM(padded, f32),
            pltpu.VMEM(padded, f32),
            pltpu.VMEM(padded, f32),
            pltpu.VMEM((2, 3, ny, nz), f32),
            pltpu.VMEM((2, 3, ny, nz), f32),
            pltpu.SemaphoreType.DMA((7,)),
            pltpu.SemaphoreType.DMA((10,)),
            pltpu.SemaphoreType.DMA((10,)),
        ],
        compiler_params=pltpu.CompilerParams(
            collective_id=0, has_side_effects=True, vmem_limit_bytes=28 * 2**20),
    )(pinned(class_porosity), step_index, pinned(checkpoint), pinned(adjoint_seed),
      pinned(material), pinned(wall_mask))
    return pl.pallas_call(
        finish,
        out_shape=(shape((19,) + cells, f32), shape(cells, f32)),
        in_specs=[vmem] * 2,
        out_specs=(anywhere, anywhere),
        scratch_shapes=[
            pltpu.SemaphoreType.DMA((5,)),
        ],
        compiler_params=pltpu.CompilerParams(vmem_limit_bytes=8 * 2**20),
    )(*kept)


def solution(mesh):
    placed = (
        P(None, "gx", "groups", None),
        P(None, "gx", "groups", None),
        P("gx", "groups", None),
        P("gx", "groups", None),
        P(),
        P("groups"),
    )
    return jax.shard_map(
        local,
        mesh=mesh,
        in_specs=placed,
        out_specs=(P(None, "gx", "groups", None), P("gx", "groups", None)),
        check_vma=False,
    )
```

```python
import functools

import jax
import jax.numpy as jnp
import numpy as np
from jax import lax
from jax.experimental import pallas as pl
from jax.experimental.pallas import tpu as pltpu
from jax.sharding import PartitionSpec as P

MESH = pl.DeviceIdType.MESH
ROWS = 8
UNROLL = 4


def velocity_list():
    rows = [(0, 0, 0)]
    for axis in range(3):
        for sign in (1, -1):
            entry = [0, 0, 0]
            entry[axis] = sign
            rows.append(tuple(entry))
    for first, second in ((0, 1), (0, 2), (1, 2)):
        for one in (1, -1):
            for two in (1, -1):
                entry = [0, 0, 0]
                entry[first] = one
                entry[second] = two
                rows.append(tuple(entry))
    return rows


VEL = velocity_list()
PLUS = [q for q in range(19) if VEL[q][0] == 1]
MINUS = [q for q in range(19) if VEL[q][0] == -1]
REST = [q for q in range(19) if VEL[q][0] == 0]
SLOT = {q: pos for pos, q in enumerate(PLUS + MINUS + REST)}
SAME = {q: q for q in range(19)}
AXIS = [(VEL.index(tuple(int(a == d) for d in range(3))),
         VEL.index(tuple(-int(a == d) for d in range(3)))) for a in range(3)]
PLANES = ((0, 1), (0, 2), (1, 2))


def corner(plane, one, two):
    entry = [0, 0, 0]
    entry[plane[0]] = one
    entry[plane[1]] = two
    return VEL.index(tuple(entry))


def to_pairs(f):
    sums = [f[p] + f[m] for p, m in AXIS]
    diffs = [f[p] - f[m] for p, m in AXIS]
    quads = []
    for plane in PLANES:
        pp, pm = f[corner(plane, 1, 1)], f[corner(plane, 1, -1)]
        mp, mm = f[corner(plane, -1, 1)], f[corner(plane, -1, -1)]
        s1, d1, s2, d2 = pp + pm, pp - pm, mp + mm, mp - mm
        quads.append((s1 + s2, d1 - d2, s1 - s2, d1 + d2))
    return f[0], sums, diffs, quads


def from_pairs(rest, sums, diffs, quads):
    out = {0: rest}
    for a, (p, m) in enumerate(AXIS):
        out[p] = sums[a] + diffs[a]
        out[m] = sums[a] - diffs[a]
    for plane, (qa, qb, qc, qd) in zip(PLANES, quads):
        s1, s2, d1, d2 = qa + qc, qa - qc, qb + qd, qd - qb
        out[corner(plane, 1, 1)] = s1 + d1
        out[corner(plane, 1, -1)] = s1 - d1
        out[corner(plane, -1, 1)] = s2 + d2
        out[corner(plane, -1, -1)] = s2 - d2
    return out


def conserved(rest, sums, diffs, quads):
    axy, axz, ayz = quads[0][0], quads[1][0], quads[2][0]
    density = (rest + (sums[0] + sums[1])) + (sums[2] + axy) + (axz + ayz)
    jx = diffs[0] + (quads[0][2] + quads[1][2])
    jy = diffs[1] + (quads[0][3] + quads[2][2])
    jz = diffs[2] + (quads[1][3] + quads[2][3])
    return density, (jx, jy, jz)


def rates(wall):
    pick = lambda at_wall, inside: jnp.where(wall, jnp.float32(at_wall), jnp.float32(inside))
    return dict(k2=pick(1, -0.6), s2=pick(0, 1.6), k3=pick(-1, -0.4), s3=pick(0, 1.4 / 3.0),
                k4=pick(1, -0.2), s4=pick(0, 1.2), sg=pick(-1, 1))


def forward(f, porosity, wall, force):
    k = rates(wall)
    rest, sums, diffs, quads = to_pairs(f)
    density, j = conserved(rest, sums, diffs, quads)
    ratio = porosity / density
    q = [porosity * c for c in j]
    u = [ratio * c for c in j]
    pxx, pyy, pzz = [q[a] * u[a] for a in range(3)]
    push = jnp.where(wall, 0.0, force)
    push3 = push * (1.0 / 3.0)
    third = density * (1.0 / 3.0)
    ninth = density * (1.0 / 9.0)
    a_of = [quads[n][0] for n in range(3)]
    even = [ninth + (pxx + pyy) * (1.0 / 3.0) - pzz * (1.0 / 6.0),
            ninth + (pxx + pzz) * (1.0 / 3.0) - pyy * (1.0 / 6.0),
            ninth + (pyy + pzz) * (1.0 / 3.0) - pxx * (1.0 / 6.0)]
    m = [sums[0] + (a_of[0] + a_of[1]), sums[1] + (a_of[0] + a_of[2]), sums[2] + (a_of[1] + a_of[2])]
    ms = [k["k2"] * m[a] + k["s2"] * (third + p) for a, p in enumerate((pxx, pyy, pzz))]
    new = []
    odd = [k["s3"] * q[0] + push3, k["s3"] * q[1], k["s3"] * q[2]]
    for n, (a, b) in enumerate(PLANES):
        qa, qb, qc, qd = quads[n]
        new.append((k["k4"] * qa + k["s4"] * even[n],
                    k["k2"] * qb + k["s2"] * (q[a] * u[b]),
                    k["k3"] * qc + odd[a],
                    k["k3"] * qd + odd[b]))
    axy, axz, ayz = new[0][0], new[1][0], new[2][0]
    s_new = [ms[0] - (axy + axz), ms[1] - (axy + ayz), ms[2] - (axz + ayz)]
    d_new = [(k["sg"] * j[0] + push) - (new[0][2] + new[1][2]),
             k["sg"] * j[1] - (new[0][3] + new[2][2]),
             k["sg"] * j[2] - (new[1][3] + new[2][3])]
    rest_new = density - (ms[0] + ms[1] + ms[2]) + (axy + axz + ayz)
    out = from_pairs(rest_new, [0.5 * s for s in s_new], [0.5 * d for d in d_new],
                     [tuple(0.25 * v for v in quad) for quad in new])
    return out, j, ratio


def backward(h, j, ratio, porosity, wall):
    k = rates(wall)
    h0, hs, hd, hq = to_pairs(h)
    hs = [0.5 * v for v in hs]
    hd = [0.5 * v for v in hd]
    hq = [tuple(0.25 * v for v in quad) for quad in hq]
    u = [ratio * c for c in j]
    ts = [v - h0 for v in hs]
    ta = [hq[n][0] - h0 - (ts[a] + ts[b]) for n, (a, b) in enumerate(PLANES)]
    tc = [(hq[n][2] - hd[a], hq[n][3] - hd[b]) for n, (a, b) in enumerate(PLANES)]
    ea = [k["s4"] * v for v in ta]
    eb = [k["s2"] * quad[1] for quad in hq]
    em = [k["s2"] * v for v in ts]
    px = em[0] + (ea[0] + ea[1]) * (1.0 / 3.0) - ea[2] * (1.0 / 6.0)
    py = em[1] + (ea[0] + ea[2]) * (1.0 / 3.0) - ea[1] * (1.0 / 6.0)
    pz = em[2] + (ea[1] + ea[2]) * (1.0 / 3.0) - ea[0] * (1.0 / 6.0)
    gx = 2.0 * px * u[0] + (eb[0] * u[1] + eb[1] * u[2])
    gy = 2.0 * py * u[1] + (eb[0] * u[0] + eb[2] * u[2])
    gz = 2.0 * pz * u[2] + (eb[1] * u[0] + eb[2] * u[1])
    a_rho = (h0 + (em[0] + em[1] + em[2]) * (1.0 / 3.0) + (ea[0] + ea[1] + ea[2]) * (1.0 / 9.0)
             - 0.5 * (u[0] * gx + u[1] * gy + u[2] * gz))
    g = [gx + k["s3"] * (tc[0][0] + tc[1][0]),
         gy + k["s3"] * (tc[0][1] + tc[2][0]),
         gz + k["s3"] * (tc[1][1] + tc[2][1])]
    grad = j[0] * g[0] + j[1] * g[1] + j[2] * g[2]
    aj = [k["sg"] * hd[a] + porosity * g[a] for a in range(3)]
    am = [k["k2"] * v for v in ts]
    quads = []
    for n, (a, b) in enumerate(PLANES):
        quads.append((k["k4"] * ta[n] + a_rho + (am[a] + am[b]),
                      k["k2"] * hq[n][1],
                      k["k3"] * tc[n][0] + aj[a],
                      k["k3"] * tc[n][1] + aj[b]))
    out = from_pairs(a_rho, [a_rho + v for v in am], aj, quads)
    return out, grad


def here(i):
    return pl.ds(pl.multiple_of(i * ROWS, ROWS), ROWS)


def walkers(ny, nz):
    steps = ny // ROWS

    def shifted(ref, slot, layer, i, sy, sz):
        row = lax.broadcasted_iota(jnp.int32, (ROWS, nz), 0)
        value = ref[slot, layer, pl.ds(pl.multiple_of(i * ROWS, ROWS), ROWS), :]
        if sy:
            near = lax.rem(i + (steps - 1 if sy > 0 else 1), steps)
            other = ref[slot, layer, pl.ds(pl.multiple_of(near * ROWS, ROWS), ROWS), :]
            value = jnp.where(row == (ROWS - 1 if sy > 0 else 0), other, value)
            value = pltpu.roll(value, sy % ROWS, 0)
        if sz:
            value = pltpu.roll(value, sz % nz, 1)
        return value

    def streamed(ref, x, i, sign, slots, without=()):
        return [jnp.zeros((ROWS, nz), jnp.float32) if VEL[q][0] in without else
                shifted(ref, slots[q], x + 1 - sign * VEL[q][0], i, sign * VEL[q][1],
                        sign * VEL[q][2]) for q in range(19)]

    def over(layers, body):
        first, stride, number = layers
        if number == 0:
            return

        def step(t, carry):
            body(first + stride * (t // steps), lax.rem(t, steps))
            return carry

        lax.fori_loop(0, number * steps, step, 0, unroll=UNROLL)

    return shifted, streamed, over


def final_body(streamed, adj, mom, por, wal, out, grad):
    def back_zero(x, i):
        at = here(i)
        h = streamed(adj, x, i, -1, SLOT)
        j = [mom[n, x, at, :] for n in range(3)]
        a, part = backward(h, j, mom[3, x, at, :], por[x, at, :], wal[x, at, :] == 1)
        for q in range(19):
            out[q, x, at, :] = a[q]
        grad[x, at, :] = grad[x, at, :] + part

    return back_zero


def near_far(axis, width):
    even = lax.rem(lax.axis_index(axis), 2) == 0
    return even, jnp.where(even, width - 1, 0), jnp.where(even, 0, width - 1)


def finish(done, part, out_hbm, grad_hbm, sem):
    copies = [pltpu.make_async_copy(done.at[pl.ds(q, min(5, 19 - q))],
                                    out_hbm.at[pl.ds(q, min(5, 19 - q))], sem.at[q // 5])
              for q in range(0, 19, 5)]
    copies.append(pltpu.make_async_copy(part, grad_hbm, sem.at[4]))
    for copy in copies:
        copy.start()
    for copy in copies:
        copy.wait()


def kernel(axis, poro_hbm, step_ref, chk_hbm, seed_hbm, mat_hbm, wall_hbm,
           out, grad, poro_ref, chk, mat, wal, mom, por, seed, post, adj, face, halo,
           load_sem, send_sem, recv_sem):
    width, ny, nz = mat.shape
    shifted, streamed, over = walkers(ny, nz)
    count = lax.axis_size(axis)
    me = lax.axis_index(axis)
    right, left = lax.rem(me + 1, count), lax.rem(me + count - 1, count)
    last = width - 1
    edge = [0, last] if width > 1 else [0]
    inner = max(width - 2, 0)

    barrier = pltpu.get_barrier_semaphore()
    for neighbour in (left, right):
        pl.semaphore_signal(barrier, inc=1, device_id={axis: neighbour}, device_id_type=MESH)

    loads = [pltpu.make_async_copy(mat_hbm, mat, load_sem.at[0]),
             pltpu.make_async_copy(wall_hbm, wal, load_sem.at[1])]
    edge_loads = [pltpu.make_async_copy(chk_hbm.at[:, x], chk.at[:, x], load_sem.at[2 + n])
                  for n, x in enumerate(edge)]
    late = []
    if inner:
        late.append(pltpu.make_async_copy(chk_hbm.at[:, pl.ds(1, inner)], chk.at[:, pl.ds(1, inner)],
                                          load_sem.at[4]))
    seed_load = pltpu.make_async_copy(seed_hbm, seed.at[:, pl.ds(1, width)], load_sem.at[5])
    loads.append(pltpu.make_async_copy(poro_hbm, poro_ref, load_sem.at[6]))
    for copy in loads + edge_loads + late + [seed_load]:
        copy.start()

    def remote(src, dst, number, target):
        return pltpu.make_async_remote_copy(
            src_ref=src, dst_ref=dst, send_sem=send_sem.at[number], recv_sem=recv_sem.at[number],
            device_id={axis: target}, device_id_type=MESH)

    seed_sends = []
    for start, size in ((1, 1), (7, 2), (11, 2)):
        seed_sends.append(remote(seed_hbm.at[pl.ds(start, size), 0],
                                 seed.at[pl.ds(start, size), width + 1], len(seed_sends), left))
    for start, size in ((2, 1), (9, 2), (13, 2)):
        seed_sends.append(remote(seed_hbm.at[pl.ds(start, size), last],
                                 seed.at[pl.ds(start, size), 0], len(seed_sends), right))
    post_up = remote(face.at[0], halo.at[0], 6, right)
    post_down = remote(face.at[1], halo.at[1], 7, left)
    adj_down = [remote(adj.at[q, 1], adj.at[q, width + 1], 8 + q, left) for q in range(5)]
    adj_up = [remote(adj.at[q, width], adj.at[q, 0], 8 + q, right) for q in range(5, 10)]

    def start(copies):
        for copy in copies:
            copy.start()

    def arrive(copies):
        for copy in copies:
            copy.wait_recv()

    bottom, top = (0, 1, 1), (last, 1, 1)
    middle = (1, 1, inner)

    def collide(x, i):
        at = here(i)
        kinds = mat[x, at, :]
        porosity = jnp.zeros((ROWS, nz), jnp.float32)
        for number in range(poro_ref.shape[0]):
            porosity = jnp.where(kinds == number, poro_ref[number], porosity)
        f = [chk[q, x, at, :] for q in range(19)]
        g, j, ratio = forward(f, porosity, wal[x, at, :] == 1, force)
        for q in range(19):
            post[SLOT[q], x + 1, at, :] = g[q]
        por[x, at, :] = porosity
        for n, value in enumerate((*j, ratio)):
            mom[n, x, at, :] = value

    def fold(x, sign):
        def body(_, i):
            moved = {VEL[q][1:]: shifted(post, SLOT[q], x + 1, i, VEL[q][1], VEL[q][2])
                     for q in (PLUS if sign > 0 else MINUS)}
            up, down, fore, aft = moved[1, 0], moved[-1, 0], moved[0, 1], moved[0, -1]
            side = 0 if sign > 0 else 1
            face[side, 0, here(i), :] = moved[0, 0] + (up + down) + (fore + aft)
            face[side, 1, here(i), :] = up - down
            face[side, 2, here(i), :] = fore - aft
        return body

    def back_one(x, i, folded=()):
        at = here(i)
        porosity = por[x, at, :]
        first = streamed(post, x, i, 1, SLOT, [sign for sign, _ in folded])
        density, j = conserved(*to_pairs(first))
        for sign, side in folded:
            total = halo[side, 0, at, :]
            density = density + total
            j = (j[0] + sign * total, j[1] + halo[side, 1, at, :], j[2] + halo[side, 2, at, :])
        h = streamed(seed, x, i, -1, SAME)
        a, part = backward(h, j, porosity / density, porosity, wal[x, at, :] == 1)
        for q in range(19):
            adj[SLOT[q], x + 1, at, :] = a[q]
        grad[x, at, :] = part

    def at_bottom(x, i):
        back_one(x, i, ((1, 0),) if width > 1 else ((1, 0), (-1, 1)))

    def at_top(x, i):
        back_one(x, i, ((-1, 1),))

    back_zero = final_body(streamed, adj, mom, por, wal, out, grad)

    turn = (step_ref[0] & 63).astype(jnp.float32) * np.float32(2.0 * np.pi / 64.0)
    force = 0.05 * jnp.sin(jnp.full((ROWS, nz), turn, jnp.float32))
    even, near, far = near_far(axis, width)

    def by_side(first, second):
        @pl.when(even)
        def _():
            first()

        second()

        @pl.when(jnp.logical_not(even))
        def _():
            first()

    def send_seeds(group):
        for copy in group:
            copy.start()

    def send_bottom():
        over(bottom, fold(0, -1))
        post_down.start()

    def send_top():
        over(top, fold(last, 1))
        post_up.start()

    pl.semaphore_wait(barrier, 2)
    by_side(lambda: send_seeds(seed_sends[:3]), lambda: send_seeds(seed_sends[3:]))
    for copy in loads + edge_loads:
        copy.wait()
    if width > 1:
        over((far, 1, 1), collide)

        @pl.when(even)
        def _():
            send_bottom()

        @pl.when(jnp.logical_not(even))
        def _():
            send_top()

        over((near, 1, 1), collide)

        @pl.when(even)
        def _():
            send_top()

        @pl.when(jnp.logical_not(even))
        def _():
            send_bottom()
    else:
        over(bottom, collide)
        send_bottom()
        send_top()
    for copy in late:
        copy.wait()
    over(middle, collide)
    seed_load.wait()
    over(middle, back_one)
    from_left, from_right = seed_sends[3:] + [post_up], seed_sends[:3] + [post_down]
    for copy in from_left if width > 1 else from_left + from_right:
        copy.wait_recv()
    over(bottom, at_bottom)
    start(adj_down)
    if width > 1:
        for copy in from_right:
            copy.wait_recv()
        over(top, at_top)
    start(adj_up)
    over(middle, back_zero)
    if width > 1:
        @pl.when(even)
        def _():
            arrive(adj_down)

        @pl.when(jnp.logical_not(even))
        def _():
            arrive(adj_up)

        over((near, 1, 1), back_zero)

        @pl.when(even)
        def _():
            arrive(adj_up)

        @pl.when(jnp.logical_not(even))
        def _():
            arrive(adj_down)

        over((far, 1, 1), back_zero)
    else:
        arrive(adj_up)
        arrive(adj_down)
        over(bottom, back_zero)
    for copy in seed_sends + [post_up, post_down] + adj_up + adj_down:
        copy.wait_send()


def local(checkpoint, adjoint_seed, material, wall_mask, class_porosity, step_index):
    width, ny, nz = material.shape
    f32 = jnp.float32
    anywhere = pl.BlockSpec(memory_space=pltpu.HBM)
    scalars = pl.BlockSpec(memory_space=pltpu.SMEM)
    vmem = pl.BlockSpec(memory_space=pltpu.VMEM)
    pinned = lambda x: pltpu.with_memory_space_constraint(x, pltpu.HBM)
    cells = (width, ny, nz)
    padded = (19, width + 2, ny, nz)
    shape = jax.ShapeDtypeStruct
    kept = pl.pallas_call(
        functools.partial(kernel, "gx"),
        out_shape=(shape((19,) + cells, f32), shape(cells, f32)),
        in_specs=[anywhere, scalars] + [anywhere] * 4,
        out_specs=(vmem,) * 2,
        scratch_shapes=[
            pltpu.SMEM(class_porosity.shape, f32),
            pltpu.VMEM((19,) + cells, f32),
            pltpu.VMEM(cells, jnp.int32),
            pltpu.VMEM(cells, jnp.int32),
            pltpu.VMEM((4,) + cells, f32),
            pltpu.VMEM(cells, f32),
            pltpu.VMEM(padded, f32),
            pltpu.VMEM(padded, f32),
            pltpu.VMEM(padded, f32),
            pltpu.VMEM((2, 3, ny, nz), f32),
            pltpu.VMEM((2, 3, ny, nz), f32),
            pltpu.SemaphoreType.DMA((7,)),
            pltpu.SemaphoreType.DMA((18,)),
            pltpu.SemaphoreType.DMA((18,)),
        ],
        compiler_params=pltpu.CompilerParams(
            collective_id=0, has_side_effects=True, vmem_limit_bytes=28 * 2**20),
    )(pinned(class_porosity), step_index, pinned(checkpoint), pinned(adjoint_seed),
      pinned(material), pinned(wall_mask))
    return pl.pallas_call(
        finish,
        out_shape=(shape((19,) + cells, f32), shape(cells, f32)),
        in_specs=[vmem] * 2,
        out_specs=(anywhere, anywhere),
        scratch_shapes=[
            pltpu.SemaphoreType.DMA((5,)),
        ],
        compiler_params=pltpu.CompilerParams(vmem_limit_bytes=8 * 2**20),
    )(*kept)


def solution(mesh):
    placed = (
        P(None, "gx", "groups", None),
        P(None, "gx", "groups", None),
        P("gx", "groups", None),
        P("gx", "groups", None),
        P(),
        P("groups"),
    )
    return jax.shard_map(
        local,
        mesh=mesh,
        in_specs=placed,
        out_specs=(P(None, "gx", "groups", None), P("gx", "groups", None)),
        check_vma=False,
    )
```
